32 devices in a mesh: space: 2 (over x), mrow: 4 (over y, core), mcol: 4 (over z).
Axes of the slice: x: 2, y: 2, z: 4, core: 2. Of those that a mesh axis runs over, the one named last changes fastest.
Arguments:
- deviation: bfloat16 [64, 48, 8192], P('space', None, ('mcol', 'mrow'))
- courant: float32 [2, 8192], P(None, ('mcol', 'mrow')), may hold values from -0.95 to 0.95
- collide: bfloat16 [8192, 8192], P('mrow', ('mcol', 'space'))
- hole_cells: int32 [768], P('space'), may hold values from -1 to 1535, as said below
- hole_wall: int32 [768], P('space'), may hold values from 0 to 3
- specular: int32 [4, 8192], replicated, may hold values from 0 to 8191, as said below
- specularity: float32 [4], replicated, may hold values from 0.2 to 0.8
Outputs:
- updated: bfloat16 [64, 48, 8192], P('space', None, ('mrow', 'mcol'))
The draws below stay inside these ranges and needn't reach their ends.
Inputs may be any that keep to these rules, and one draw needn't show every extreme that they name: `hole_cells`: within one tile the used slots come first and name distinct cells; every tile has at least 96 used slots, some tile has all 384 slots used and some tile has an empty slot. Each row specular[w] is a permutation of the modes; for an outgoing mode i of aligned block e = i // 512, its incoming mode j lies, within j's own aligned block of 512 modes, in the sub-block of 32 modes numbered e, that is (j % 512) // 32 == e.
All inputs are finite; a program needn't handle non-finite values.
Results may differ from the reference program's by a relative error of at most 0.005.
Values may be sent and summed in bfloat16 or wider, within the bound.
No kernel may reach another device: no remote copies, remote signals or barrier semaphores. Data moves between devices by JAX's collectives and lax.ppermute only.
A program may use at most 128 MiB of HBM per device.

```python
import math
import jax
import jax.numpy as jnp
from jax import lax

M = 8192
NW = 4
CX = 32
CY = 48
BMAX = 384
NX = 64
N_SPACE = 2
N_MROW = 4
N_MCOL = 4


def draw_deviation(key, part):
    key_off, key_noise, key_scale = jax.random.split(key, 3)
    offset = jax.random.uniform(key_off, (NX, CY, 1), jnp.float32, -1.0, 1.0)
    scales = jnp.exp(jax.random.uniform(key_scale, (1, 1, M), jnp.float32, math.log(0.3), math.log(3.0)))
    noise = jnp.clip(jax.random.normal(key_noise, (NX, CY, M), jnp.float32), -4.0, 4.0)
    return (offset + scales * noise).astype(jnp.bfloat16)


def draw_collide(key, part):
    key_off, key_diag = jax.random.split(key, 2)
    spread = 0.5 * jnp.clip(jax.random.normal(key_off, (M, M), jnp.float32), -4.0, 4.0) / math.sqrt(M)
    diagonal = jax.random.uniform(key_diag, (M, 1), jnp.float32, 0.3, 0.9)
    row_ids = jnp.arange(M, dtype=jnp.int32)[:, None]
    col_ids = jnp.arange(M, dtype=jnp.int32)[None, :]
    return jnp.where(row_ids == col_ids, diagonal, spread).astype(jnp.bfloat16)


def draw_hole_cells(key, part):
    key_perm, key_count, key_pick, key_slot = jax.random.split(key, 4)
    tile_cells = CX * CY
    tile_keys = jax.random.split(key_perm, N_SPACE)
    orders = jax.vmap(lambda single: jax.random.permutation(single, tile_cells - 1))(tile_keys)[:, :BMAX]
    forced = jax.random.randint(key_pick, (), 0, N_SPACE)
    chosen_slot = jax.random.randint(key_slot, (), 0, BMAX)
    slot_ids = jnp.arange(BMAX, dtype=jnp.int32)
    tile_ids = jnp.arange(N_SPACE, dtype=jnp.int32)
    orders = jnp.where((tile_ids[:, None] == forced) & (slot_ids[None, :] == chosen_slot), tile_cells - 1, orders)
    counts = jax.random.randint(key_count, (N_SPACE,), BMAX // 4, BMAX)
    counts = jnp.where(tile_ids == forced, BMAX, counts)
    return jnp.where(slot_ids[None, :] < counts[:, None], orders, -1).reshape(-1).astype(jnp.int32)


def draw_specular(key, part):
    groups = N_MROW * N_MCOL
    block = M // groups
    sub = block // groups
    key_shift, key_off = jax.random.split(jax.random.fold_in(key, 17))
    shift_keys = jax.random.split(key_shift, NW)
    sigma = jax.vmap(lambda single: jax.random.permutation(single, groups))(shift_keys).astype(jnp.int32)
    offsets = jax.random.randint(key_off, (NW, groups, groups), 0, sub).astype(jnp.int32)
    modes = jnp.arange(M, dtype=jnp.int32)
    dest_block = modes // block
    sub_index = modes % block // sub
    within = modes % sub
    source_block = (dest_block[None, :] + sigma[:, sub_index]) % groups
    source_within = (within[None, :] + offsets[:, dest_block, sub_index]) % sub
    return (source_block * block + dest_block[None, :] * sub + source_within).astype(jnp.int32)


def place_ends(values, own_key, least, top_value):
    dims = values.shape
    index_at = [jax.random.randint(jax.random.fold_in(own_key, axis), (), 0, dims[axis]) for axis in range(len(dims))]
    values = values.at[tuple(index_at)].set(least)
    longest = dims.index(max(dims))
    index_at[longest] = (index_at[longest] + 1) % dims[longest]
    return values.at[tuple(index_at)].set(top_value)


def steps_of(key, extent, pieces, smallest, high):
    def one(axis_at, blocks):
        steps = jax.random.uniform(jax.random.fold_in(jax.random.fold_in(key, 6), axis_at), (blocks,), jnp.float32, smallest / len(pieces), high / len(pieces))
        return jnp.repeat(jnp.exp(steps), extent[axis_at] // blocks).reshape((-1,) + (1,) * (len(extent) - axis_at - 1))

    level = one(*pieces[0])
    for cut in pieces[1:]:
        level = level * one(*cut)
    return level


def setup_inputs(seed: int = 0) -> dict:
    streams_of = jax.random.split(jax.random.key(seed), 8)
    deviation = draw_deviation(jax.random.fold_in(streams_of[7], 71), 0)
    courant = jnp.clip(jax.random.uniform(streams_of[1], (2, M), jnp.float32, -0.95, 0.95) * steps_of(streams_of[1], (2, M), ((1, 16),), -0.4, 0.0), -0.95, 0.95)
    collide = draw_collide(jax.random.fold_in(streams_of[7], 71), 0)
    hole_cells = draw_hole_cells(jax.random.fold_in(streams_of[7], 71), 0)
    hole_wall = place_ends(jax.random.randint(streams_of[4], (N_SPACE * BMAX,), 0, NW), jax.random.fold_in(streams_of[4], 1), 0, NW - 1).astype(jnp.int32)
    specular = draw_specular(jax.random.fold_in(streams_of[7], 71), 0)
    specularity = jnp.clip(jax.random.uniform(streams_of[6], (NW,), jnp.float32, 0.2, 0.8), 0.2, 0.8)
    return dict(deviation=deviation, courant=courant, collide=collide, hole_cells=hole_cells, hole_wall=hole_wall, specular=specular, specularity=specularity)


def upwind(padded, courant):
    field = padded.astype(jnp.float32)
    reach_x = jnp.abs(courant[0])
    reach_y = jnp.abs(courant[1])
    center = field[1:-1]
    upwind_x = jnp.where(courant[0] > 0, field[:-2], field[2:])
    upwind_y = jnp.where(courant[1] > 0, jnp.roll(center, 1, axis=1), jnp.roll(center, -1, axis=1))
    upwind_xy = jnp.where(courant[1] > 0, jnp.roll(upwind_x, 1, axis=1), jnp.roll(upwind_x, -1, axis=1))
    result = (1.0 - reach_x) * (1.0 - reach_y) * center + reach_x * (1.0 - reach_y) * upwind_x
    result = result + (1.0 - reach_x) * reach_y * upwind_y + reach_x * reach_y * upwind_xy
    return result.astype(jnp.bfloat16)


def reference(deviation, courant, collide, hole_cells, hole_wall, specular, specularity):
    length_x, width_y, modes = deviation.shape
    block_len = min(512, modes)
    block_count = modes // block_len
    blocks = deviation.reshape(length_x, width_y, block_count, block_len).transpose(2, 0, 1, 3)
    speeds = courant.reshape(2, block_count, block_len).transpose(1, 0, 2)

    def stream_block(pair):
        part_dev, part_speed = pair
        padded = jnp.pad(part_dev, ((1, 1), (0, 0), (0, 0)))
        return upwind(padded, part_speed)

    read = lax.map(stream_block, (blocks, speeds))
    read = read.transpose(1, 2, 0, 3).reshape(length_x * width_y, modes)
    tile_cells = CX * CY
    tile_ids = jnp.arange(hole_cells.shape[0], dtype=jnp.int32) // BMAX
    is_live = hole_cells >= 0
    global_ids = jnp.where(is_live, tile_ids * tile_cells + hole_cells, 0).astype(jnp.int32)
    rim_rows = read[global_ids]
    diffuse = jnp.sum(rim_rows.astype(jnp.float32), axis=1) / modes
    source_modes = specular[hole_wall]
    mirrored = jnp.take_along_axis(rim_rows, source_modes, axis=1).astype(jnp.float32)
    share = specularity[hole_wall][:, None]
    emitted = (share * mirrored + (1.0 - share) * diffuse[:, None]).astype(jnp.bfloat16)
    target_ids = jnp.where(is_live, global_ids, length_x * width_y).astype(jnp.int32)
    reemitted = read.at[target_ids].set(emitted, mode="drop")
    product = lax.dot_general(reemitted, collide, (((1,), (1,)), ((), ())), preferred_element_type=jnp.float32)
    return product.astype(jnp.bfloat16).reshape(length_x, width_y, modes)
```

```python
import functools
import jax
import jax.numpy as jnp
import numpy as np
from jax import lax
from jax.experimental import pallas as pl
from jax.experimental.pallas import tpu as pltpu
from jax.sharding import PartitionSpec as P

VMEM = pltpu.VMEM
SMEM = pltpu.SMEM
ANY = pl.ANY
NT = (((1,), (1,)), ((), ()))
LIMIT = 48 * 1024 * 1024
CELL_CHUNKS = 3
TAIL = 16


def line_steps(size):
    order = []
    for c in range(size):
        row = []
        for t in range(1, size):
            if c <= t - 1:
                row.append(c + size - t)
            if c >= size - t:
                row.append(c - size + t)
        row.append(c)
        order.append(row)
    return np.array(order, np.int32)


def slot_of(c, t, size):
    place = 0
    for u in range(1, t):
        place = place + jnp.where(c <= u - 1, 1, 0) + jnp.where(c >= size - u, 1, 0)
    return place


def slots_at(t, size):
    found = set()
    for c in range(size):
        place = 0
        for u in range(1, size):
            for hit in (c <= u - 1, c >= size - u):
                if hit:
                    if u == t:
                        found.add(place)
                    place += 1
        if t == size:
            found.add(size - 1)
    return sorted(found)


def read_kernel(rows_of, cols_of, dev, before, after, courant, select, read, payload):
    width_x, width_y, modes = dev.shape
    speed = courant[...]
    reach = jnp.abs(speed)
    ahead = speed > 0
    a = jnp.broadcast_to(reach[0:1], (width_y, modes))
    b = jnp.broadcast_to(reach[1:2], (width_y, modes))
    ahead_x = jnp.broadcast_to(ahead[0:1], (width_y, modes))
    ahead_y = jnp.broadcast_to(ahead[1:2], (width_y, modes))

    def one(x, low, high):
        center = dev[x].astype(jnp.float32)
        ux = jnp.where(ahead_x, low.astype(jnp.float32), high.astype(jnp.float32))
        along = (1.0 - a) * center + a * ux
        shifted = jnp.where(ahead_y, pltpu.roll(along, 1, 0), pltpu.roll(along, width_y - 1, 0))
        read[pl.ds(pl.multiple_of(x * width_y, 16), width_y), :] = (
            (1.0 - b) * along + b * shifted
        ).astype(read.dtype)

    one(0, before[0], dev[1])

    def body(x, carry):
        one(x, dev[x - 1], dev[x + 1])
        return carry

    lax.fori_loop(1, width_x - 1, body, 0)
    one(width_x - 1, dev[width_x - 2], after[0])

    rim = lax.dot_general(
        select[...], read[...], (((1,), (0,)), ((), ())), preferred_element_type=jnp.float32
    )
    flipped = rim.T
    total = jnp.sum(flipped, axis=0, keepdims=True)
    high = total.astype(jnp.bfloat16).astype(jnp.float32)
    middle = (total - high).astype(jnp.bfloat16).astype(jnp.float32)
    low = total - high - middle
    place = lax.broadcasted_iota(jnp.int32, (TAIL, total.shape[1]), 0)
    tail = jnp.where(place == 0, high, jnp.where(place == 1, middle, jnp.where(place == 2, low, 0.0)))
    tail = tail.astype(jnp.bfloat16)
    piece = modes // (rows_of * cols_of)
    packed = flipped.astype(jnp.bfloat16)
    for r in range(rows_of):
        for c in range(cols_of):
            block = c * rows_of + r
            payload[r * cols_of + c, 0:piece, :] = packed[block * piece : (block + 1) * piece]
            payload[r * cols_of + c, piece : piece + TAIL, :] = tail


def rim_kernel(mode_count, specularity, read, arrived, mirror, place, on_rim, wall, *outs):
    groups, height, slots = arrived.shape
    piece = height - TAIL
    values = arrived[:, 0:piece, :].reshape(groups * piece, slots)
    sums = arrived[:, piece:height, :].reshape(groups * TAIL, slots).astype(jnp.float32)
    diffuse = jnp.sum(sums, axis=0, keepdims=True) / mode_count
    walls = wall[...]
    share = jnp.zeros(walls.shape, jnp.float32)
    mirrored = jnp.zeros((groups * piece, slots), jnp.float32)
    for w in range(mirror.shape[0]):
        share = jnp.where(walls == w, specularity[w], share)
        picked = lax.dot_general(
            mirror[w], values, (((1,), (0,)), ((), ())), preferred_element_type=jnp.float32
        )
        mirrored = jnp.where(walls == w, picked, mirrored)
    emitted = (share * mirrored + (1.0 - share) * diffuse).astype(jnp.bfloat16)
    step = outs[0].shape[0]
    for n, out in enumerate(outs):
        rows = slice(n * step, (n + 1) * step)
        spread = lax.dot_general(place[rows, :], emitted, NT, preferred_element_type=jnp.float32)
        out[...] = jnp.where(on_rim[rows, :] > 0, spread, read[rows, :].astype(jnp.float32)).astype(
            out.dtype
        )


def hop_kernel(t, size, wide, slots, has_recv, *refs):
    refs = list(refs)
    where = refs.pop(0)
    blocks = [refs.pop(0) for _ in range(4)]
    own = refs.pop(0)
    others = {j: refs.pop(0) for j in slots}
    final = t == size
    recv = [refs.pop(0), refs.pop(0)] if has_recv else None
    outs = [refs.pop(0)] if final else [refs.pop(0), refs.pop(0)]
    buffer, sem = refs
    s, r, c = where[0], where[1], where[2]
    rows = buffer.shape[1]
    width = blocks[0].shape[1]
    if final:
        jobs = [(c, None, size - 1)]
    else:
        first = slot_of(c, t, size)
        goes_right = c <= t - 1
        jobs = [
            (c + size - t, goes_right, first),
            (c - size + t, c >= size - t, first + jnp.where(goes_right, 1, 0)),
        ]

    def fetch(n, d, place):
        for b in range(4):
            source = lax.bitwise_xor(r, b)
            target = buffer.at[n, :, b * width : (b + 1) * width]
            if wide:
                column = pl.multiple_of(source * width, width)
                pltpu.make_async_copy(
                    own.at[pl.ds(pl.multiple_of(d * rows, rows), rows), pl.ds(column, width)],
                    target,
                    sem.at[n],
                ).start()
                continue
            column = pl.multiple_of(lax.bitwise_and(source, 1) * width, width)
            is_own = lax.shift_right_logical(source, 1) == s

            @pl.when(is_own)
            def _():
                pltpu.make_async_copy(
                    own.at[pl.ds(pl.multiple_of(d * rows, rows), rows), pl.ds(column, width)],
                    target,
                    sem.at[n],
                ).start()

            for j, other in others.items():

                @pl.when(jnp.logical_and(jnp.logical_not(is_own), place == j))
                def _(other=other):
                    pltpu.make_async_copy(other.at[:, pl.ds(column, width)], target, sem.at[n]).start()

    def multiply(n, out):
        pltpu.make_async_copy(buffer.at[n], buffer.at[n], sem.at[n]).wait()
        total = None
        for b in range(4):
            part = lax.dot_general(
                blocks[b][...],
                buffer[n, :, b * width : (b + 1) * width],
                NT,
                preferred_element_type=jnp.float32,
            )
            total = part if total is None else total + part
        if final:
            total = total + recv[0][...].astype(jnp.float32) + recv[1][...].astype(jnp.float32)
        elif has_recv:
            total = total + recv[n][...].astype(jnp.float32)
        out[...] = total.astype(out.dtype)

    for n, (d, valid, place) in enumerate(jobs):
        if valid is None:
            fetch(n, d, place)
        else:
            pl.when(valid)(functools.partial(fetch, n, d, place))
    for n, (d, valid, place) in enumerate(jobs):
        if valid is None:
            multiply(n, outs[n])
        else:
            pl.when(valid)(functools.partial(multiply, n, outs[n]))


def hop(t, size, wide, where, blocks, own, others, recv):
    slots = () if wide else tuple(slots_at(t, size))
    rows = own.shape[0] // size
    cells, width = blocks[0].shape
    count = 1 if t == size else 2
    spec = pl.BlockSpec(memory_space=VMEM)
    any_spec = pl.BlockSpec(memory_space=ANY)
    operands = [where, *blocks, own, *[others[j] for j in slots], *(recv or [])]
    in_specs = [pl.BlockSpec(memory_space=SMEM)] + [spec] * 4 + [any_spec] * (1 + len(slots))
    in_specs += [spec] * len(recv or [])
    return pl.pallas_call(
        functools.partial(hop_kernel, t, size, wide, slots, recv is not None),
        out_shape=[jax.ShapeDtypeStruct((cells, rows), jnp.bfloat16)] * count,
        in_specs=in_specs,
        out_specs=[spec] * count,
        scratch_shapes=[
            pltpu.VMEM((count, rows, 4 * width), jnp.bfloat16),
            pltpu.SemaphoreType.DMA((count,)),
        ],
        compiler_params=pltpu.CompilerParams(vmem_limit_bytes=LIMIT),
        cost_estimate=pl.CostEstimate(
            flops=2 * cells * rows * width * 4, bytes_accessed=8 * cells * width * 2, transcendentals=0
        ),
    )(*operands)


def on_device(deviation, courant, collide, hole_cells, hole_wall, specular, specularity):
    n_space, n_row, n_col = (lax.axis_size(name) for name in ("space", "mrow", "mcol"))
    s, r, c = (lax.axis_index(name) for name in ("space", "mrow", "mcol"))
    width_x, width_y, block_len = deviation.shape
    cell_count = width_x * width_y
    slot_count = hole_cells.shape[0]
    wall_count, mode_count = specular.shape
    piece = block_len // (n_row * n_col)
    groups = n_row * n_col
    vmem = pl.BlockSpec(memory_space=VMEM)
    params = pltpu.CompilerParams(vmem_limit_bytes=LIMIT)
    where = jnp.stack([s, r, c]).astype(jnp.int32)

    up = [(i, i + 1) for i in range(n_space - 1)]
    down = [(j, i) for i, j in up]
    before = lax.ppermute(deviation[-1:], "space", up)
    after = lax.ppermute(deviation[:1], "space", down)

    cells = jnp.arange(cell_count, dtype=jnp.int32)
    select = (hole_cells[:, None] == cells[None, :]).astype(jnp.bfloat16)
    place = (cells[:, None] == hole_cells[None, :]).astype(jnp.bfloat16)
    on_rim = jnp.max(place.astype(jnp.float32), axis=1, keepdims=True)
    own_table = lax.dynamic_slice_in_dim(specular, (c * n_row + r) * block_len, block_len, 1)
    source = own_table // block_len
    positions = (source % n_row * n_col + source // n_row) * piece + own_table % piece
    mirror = (
        positions[:, :, None] == jnp.arange(block_len, dtype=jnp.int32)[None, None, :]
    ).astype(jnp.bfloat16)

    wide = n_space != 2
    rows = collide.shape[0] // n_col
    others = []
    if wide:
        own = lax.all_gather(collide, "space", axis=1, tiled=True)
    else:
        own = collide
        order = jnp.asarray(line_steps(n_col))
        token = (before, after)
        for j in range(n_col):
            part = lax.dynamic_slice_in_dim(collide, order[c, j] * rows, rows, 0)
            part, token = lax.optimization_barrier((part, token))
            got = lax.ppermute(part, "space", [(0, 1), (1, 0)])
            others.append(got)
            token = got
            if j == 0:
                before, after = before, after

    read, payload = pl.pallas_call(
        functools.partial(read_kernel, n_row, n_col),
        out_shape=[
            jax.ShapeDtypeStruct((cell_count, block_len), jnp.bfloat16),
            jax.ShapeDtypeStruct((groups, piece + TAIL, slot_count), jnp.bfloat16),
        ],
        in_specs=[vmem] * 5,
        out_specs=[vmem] * 2,
        compiler_params=params,
    )(deviation, before, after, courant, select)
    arrived = lax.all_to_all(payload, ("mrow", "mcol"), split_axis=0, concat_axis=0, tiled=True)
    step = cell_count // CELL_CHUNKS
    own_chunks = pl.pallas_call(
        functools.partial(rim_kernel, mode_count),
        out_shape=[jax.ShapeDtypeStruct((step, block_len), jnp.bfloat16)] * CELL_CHUNKS,
        in_specs=[pl.BlockSpec(memory_space=SMEM)] + [vmem] * 6,
        out_specs=[vmem] * CELL_CHUNKS,
        compiler_params=params,
    )(specularity, read, arrived, mirror, place, on_rim, hole_wall[None, :])

    flip = [[(i, i ^ bit) for i in range(n_row)] for bit in (1, 2)]
    chunks = []
    for mine in own_chunks:
        far = lax.ppermute(mine, "mrow", flip[1])
        near = lax.ppermute(mine, "mrow", flip[0])
        both = lax.ppermute(far, "mrow", flip[0])
        chunks.append([mine, near, far, both])

    right = [(i, i + 1) for i in range(n_col - 1)]
    left = [(j, i) for i, j in right]
    state = [None] * CELL_CHUNKS
    for t in range(1, n_col):
        for n in range(CELL_CHUNKS):
            to_right, to_left = hop(t, n_col, wide, where, chunks[n], own, others, state[n])
            state[n] = [
                lax.ppermute(to_right, "mcol", right[:t]),
                lax.ppermute(to_left, "mcol", left[n_col - 1 - t :]),
            ]
    outs = [
        hop(n_col, n_col, wide, where, chunks[n], own, others, state[n])[0] for n in range(CELL_CHUNKS)
    ]
    return jnp.concatenate(outs, axis=0).reshape(width_x, width_y, rows)


def solution(mesh):
    in_specs = (
        P("space", None, ("mcol", "mrow")),
        P(None, ("mcol", "mrow")),
        P("mrow", ("mcol", "space")),
        P("space"),
        P("space"),
        P(),
        P(),
    )
    out_specs = P("space", None, ("mrow", "mcol"))
    return jax.shard_map(
        on_device, mesh=mesh, in_specs=in_specs, out_specs=out_specs, check_vma=False
    )
```

```python
import functools
import jax
import jax.numpy as jnp
import numpy as np
from jax import lax
from jax.experimental import pallas as pl
from jax.experimental.pallas import tpu as pltpu
from jax.sharding import PartitionSpec as P

SMEM = pltpu.SMEM
HBM = pltpu.HBM
NT = (((1,), (1,)), ((), ()))
SPLIT = (2, 1)
LIMIT = 60 * 1024 * 1024
HOP_LIMIT = 16 * 1024 * 1024


def takes(microseconds):
    return pl.CostEstimate(flops=int(microseconds * 0.5e9), bytes_accessed=0, transcendentals=0)


TAIL = 16


def line_steps(size):
    order = []
    for c in range(size):
        row = []
        for t in range(1, size):
            if c <= t - 1:
                row.append(c + size - t)
            if c >= size - t:
                row.append(c - size + t)
        row.append(c)
        order.append(row)
    return np.array(order, np.int32)


def slot_of(c, t, size):
    place = 0
    for u in range(1, t):
        place = place + jnp.where(c <= u - 1, 1, 0) + jnp.where(c >= size - u, 1, 0)
    return place


def slots_at(t, size):
    found = set()
    for c in range(size):
        place = 0
        for u in range(1, size):
            for hit in (c <= u - 1, c >= size - u):
                if hit:
                    if u == t:
                        found.add(place)
                    place += 1
        if t == size:
            found.add(size - 1)
    return sorted(found)


def moves(lane, head, fill, spare, on_rim):
    slots = lane.shape[1]
    sub = jnp.broadcast_to(lane, (128, slots)).T[:, 0:1]
    total = jnp.sum((lane >= 0).astype(jnp.float32), axis=1, keepdims=True).astype(jnp.int32)
    in_head = jnp.logical_and(lane >= 0, lane < head)
    head_count = jnp.sum(in_head.astype(jnp.float32), axis=1, keepdims=True).astype(jnp.int32)
    place = lax.broadcasted_iota(jnp.int32, (1, slots), 1)
    tail = jnp.broadcast_to(place + head, (slots, slots))
    wide_sub = jnp.broadcast_to(sub, (slots, slots))
    before = jnp.logical_and(wide_sub >= head, wide_sub < tail).astype(jnp.float32)
    hit = (wide_sub == tail).astype(jnp.float32)
    rank = place - jnp.sum(before, axis=0, keepdims=True).astype(jnp.int32)
    tail_key = jnp.where(jnp.sum(hit, axis=0, keepdims=True) > 0, -2, rank)
    row = lax.broadcasted_iota(jnp.int32, (head, slots), 0)
    wide_lane = jnp.broadcast_to(lane, (head, slots))
    ahead = jnp.logical_and(wide_lane >= 0, wide_lane < row).astype(jnp.float32)
    hits = jnp.max((wide_lane == row).astype(jnp.float32), axis=1, keepdims=True)
    head_key = jnp.where(hits > 0, jnp.sum(ahead, axis=1, keepdims=True).astype(jnp.int32), -1)
    on_rim[...] = hits
    fill[...] = (head_key == tail_key).astype(jnp.float32).astype(jnp.bfloat16)
    slot = lax.broadcasted_iota(jnp.int32, (slots, 1), 0)
    slot_key = jnp.where(slot >= total, slot - total + head_count, -1)
    spare[...] = (slot_key == tail_key).astype(jnp.float32).astype(jnp.bfloat16)
    return sub


def late_mask_kernel(rows_of, cols_of, cells_lane, table, mirror, place, fill, spare, on_rim):
    cell = lax.broadcasted_iota(jnp.int32, place.shape, 0)
    place[...] = (cells_lane[...] == cell).astype(jnp.float32).astype(jnp.bfloat16)
    modes = mirror.shape[1]
    piece = modes // (rows_of * cols_of)
    entry = table[...]
    block = lax.div(entry, modes)
    group = lax.rem(block, rows_of) * cols_of + lax.div(block, rows_of)
    position = group * piece + lax.rem(entry, piece)
    source = lax.broadcasted_iota(jnp.int32, mirror.shape[1:], 0)
    for w in range(mirror.shape[0]):
        mirror[w] = (position[w : w + 1] == source).astype(jnp.float32).astype(jnp.bfloat16)
    moves(cells_lane[...], fill.shape[0], fill, spare, on_rim)


def pick_kernel(where, table, whole, out, sem):
    rows = out.shape[0]
    first = pl.multiple_of(table[where[2], 0] * rows, rows)
    copy = pltpu.make_async_copy(whole.at[pl.ds(first, rows), :], out, sem)
    copy.start()
    copy.wait()


def read_kernel(rows_of, cols_of, count, shards, *refs):
    refs = list(refs)
    dev, before, after, courant, cells_lane = (refs.pop(0) for _ in range(5))
    where, table, whole = (refs.pop(0) for _ in range(3)) if shards else (None, None, None)
    payload, extra = refs.pop(0), refs.pop(0)
    outs = [refs.pop(0) for _ in range(count)]
    parts = [refs.pop(0) for _ in range(shards)]
    read, select, fill, spare, on_rim = (refs.pop(0) for _ in range(5))
    fetches, stores = [], []
    if shards:
        stage, in_sem, out_sem = refs
        rows = stage.shape[1]
        for j in range(shards):
            first = pl.multiple_of(table[where[2], j + 1] * rows, rows)
            fetches.append(
                pltpu.make_async_copy(whole.at[pl.ds(first, rows), :], stage.at[j], in_sem.at[j])
            )
            stores.append(pltpu.make_async_copy(stage.at[j], parts[j], out_sem.at[j]))
    for copy in fetches:
        copy.start()
    sub = moves(cells_lane[...], fill.shape[0], fill, spare, on_rim)
    cell = lax.broadcasted_iota(jnp.int32, select.shape, 1)
    select[...] = (sub == cell).astype(jnp.float32).astype(jnp.bfloat16)
    width_x, width_y, modes = dev.shape
    speed = courant[...]
    reach = jnp.abs(speed)
    ahead = speed > 0
    a = jnp.broadcast_to(reach[0:1], (width_y, modes))
    b = jnp.broadcast_to(reach[1:2], (width_y, modes))
    ahead_x = jnp.broadcast_to(ahead[0:1], (width_y, modes))
    ahead_y = jnp.broadcast_to(ahead[1:2], (width_y, modes))

    def one(x, low, high):
        center = dev[x].astype(jnp.float32)
        ux = jnp.where(ahead_x, low.astype(jnp.float32), high.astype(jnp.float32))
        along = (1.0 - a) * center + a * ux
        shifted = jnp.where(ahead_y, pltpu.roll(along, 1, 0), pltpu.roll(along, width_y - 1, 0))
        read[pl.ds(pl.multiple_of(x * width_y, 16), width_y), :] = (
            (1.0 - b) * along + b * shifted
        ).astype(read.dtype)

    one(0, before[0], dev[1])

    def body(x, carry):
        one(x, dev[x - 1], dev[x + 1])
        return carry

    lax.fori_loop(1, width_x - 1, body, 0)
    one(width_x - 1, dev[width_x - 2], after[0])

    for fetch, store in zip(fetches, stores):
        fetch.wait()
        store.start()
    head = read.shape[0] - extra.shape[0]
    tail_rows = read[head:, :]
    first = 0
    for out in outs:
        rows = slice(first, first + out.shape[0])
        first += out.shape[0]
        moved = jnp.dot(fill[rows, :], tail_rows, preferred_element_type=jnp.float32)
        kept = read[rows, :].astype(jnp.float32)
        out[...] = jnp.where(on_rim[rows, :] > 0, moved, kept).astype(out.dtype)
    extra[...] = jnp.dot(spare[...], tail_rows, preferred_element_type=jnp.float32).astype(extra.dtype)

    rim = jnp.dot(select[...], read[...], preferred_element_type=jnp.float32)
    flipped = rim.T
    total = jnp.sum(flipped, axis=0, keepdims=True)
    high = total.astype(jnp.bfloat16).astype(jnp.float32)
    middle = (total - high).astype(jnp.bfloat16).astype(jnp.float32)
    low = total - high - middle
    place = lax.broadcasted_iota(jnp.int32, (TAIL, total.shape[1]), 0)
    tail = jnp.where(place == 0, high, jnp.where(place == 1, middle, jnp.where(place == 2, low, 0.0)))
    tail = tail.astype(jnp.bfloat16)
    piece = modes // (rows_of * cols_of)
    packed = flipped.astype(jnp.bfloat16)
    for r in range(rows_of):
        for c in range(cols_of):
            block = c * rows_of + r
            payload[r * cols_of + c, 0:piece, :] = packed[block * piece : (block + 1) * piece]
            payload[r * cols_of + c, piece : piece + TAIL, :] = tail
    for store in stores:
        store.wait()


def rim_kernel(mode_count, specularity, arrived, mirror, wall, cells_lane, extra, out):
    groups, height, slots = arrived.shape
    piece = height - TAIL
    values = arrived[:, 0:piece, :].reshape(groups * piece, slots).T
    sums = arrived[:, piece:height, :].reshape(groups * TAIL, slots).astype(jnp.float32)
    total = jnp.broadcast_to(jnp.sum(sums, axis=0, keepdims=True), (128, slots)).T
    diffuse = total[:, 0:1] / mode_count
    walls = jnp.broadcast_to(wall[...], (128, slots)).T[:, 0:1]
    share = jnp.zeros(walls.shape, jnp.float32)
    mirrored = jnp.zeros(out.shape, jnp.float32)
    for w in range(mirror.shape[0]):
        share = jnp.where(walls == w, specularity[w], share)
        picked = jnp.dot(values, mirror[w], preferred_element_type=jnp.float32)
        mirrored = jnp.where(walls == w, picked, mirrored)
    emitted = share * mirrored + (1.0 - share) * diffuse
    used = jnp.broadcast_to(cells_lane[...], (128, slots)).T[:, 0:1] >= 0
    out[...] = jnp.where(used, emitted, extra[...].astype(jnp.float32)).astype(out.dtype)


def ends_kernel(fill, *refs):
    parts, ends = refs[:-1], refs[-1]
    total, first = None, 0
    for part in parts:
        rows = slice(first, first + part.shape[0])
        first += part.shape[0]
        moved = lax.dot_general(
            fill[rows, :], part[...], (((0,), (0,)), ((), ())), preferred_element_type=jnp.float32
        )
        total = moved if total is None else total + moved
    ends[...] = total


def merge_kernel(fill, spare, place, on_rim, ends, total, from_left, from_right, *refs):
    parts, out = refs[:-1], refs[-1]
    head = on_rim.shape[0]
    slots = spare.shape[0]
    total = total[...] + from_left[...].astype(jnp.float32) + from_right[...].astype(jnp.float32)
    total = total.astype(jnp.bfloat16)
    kept = total.shape[0] - slots
    last = total[kept:, :]
    parts = [part[...] for part in parts] + [total[:kept, :]]
    tn = (((0,), (0,)), ((), ()))
    back = lax.dot_general(spare[...], last, tn, preferred_element_type=jnp.float32)
    back = back + jnp.dot(place[head:, :], last, preferred_element_type=jnp.float32)
    back = back + lax.dot_general(
        fill[head - kept :, :], parts[-1], tn, preferred_element_type=jnp.float32
    )
    out[head:, :] = (back + ends[...]).astype(out.dtype)
    first = 0
    for part in parts:
        rows = slice(first, first + part.shape[0])
        first += part.shape[0]
        moved = jnp.dot(place[rows, :], last, preferred_element_type=jnp.float32)
        out[rows, :] = jnp.where(on_rim[rows, :] > 0, moved, part.astype(jnp.float32)).astype(out.dtype)


def hop_kernel(t, size, wide, slots, groups, has_recv, *refs):
    refs = list(refs)
    where = refs.pop(0)
    blocks = [[refs.pop(0) for _ in range(4)] for _ in range(groups)]
    own = refs.pop(0) if wide else None
    held = {j: (refs.pop(0), refs.pop(0)) for j in slots}
    final = t == size
    recv = [refs.pop(0), refs.pop(0)] if has_recv else None
    outs = [refs.pop(0)] if final else [refs.pop(0), refs.pop(0)]
    buffer, sem = refs
    s, r, c = where[0], where[1], where[2]
    rows = buffer.shape[1]
    width = blocks[0][0].shape[1]
    if final:
        jobs = [(c, None, size - 1)]
    else:
        first = slot_of(c, t, size)
        goes_right = c <= t - 1
        jobs = [
            (c + size - t, goes_right, first),
            (c - size + t, c >= size - t, first + jnp.where(goes_right, 1, 0)),
        ]

    def fetch(n, d, place):
        for b in range(4):
            source = lax.bitwise_xor(r, b)
            target = buffer.at[n, :, b * width : (b + 1) * width]
            if wide:
                column = pl.multiple_of(source * width, width)
                pltpu.make_async_copy(
                    own.at[pl.ds(pl.multiple_of(d * rows, rows), rows), pl.ds(column, width)],
                    target,
                    sem.at[n],
                ).start()
                continue
            column = pl.multiple_of(lax.bitwise_and(source, 1) * width, width)
            is_own = lax.shift_right_logical(source, 1) == s
            for j, pair in held.items():
                for use, shard in ((is_own, pair[0]), (jnp.logical_not(is_own), pair[1])):

                    @pl.when(jnp.logical_and(use, place == j))
                    def _(shard=shard):
                        pltpu.make_async_copy(shard.at[:, pl.ds(column, width)], target, sem.at[n]).start()

    def multiply(n, out):
        pltpu.make_async_copy(buffer.at[n], buffer.at[n], sem.at[n]).wait()
        first = 0
        for group in blocks:
            rows_here = slice(first, first + group[0].shape[0])
            first += group[0].shape[0]
            total = None
            for b in range(4):
                part = lax.dot_general(
                    group[b][...],
                    buffer[n, :, b * width : (b + 1) * width],
                    NT,
                    preferred_element_type=jnp.float32,
                )
                total = part if total is None else total + part
            if final and has_recv:
                total = total + recv[0][rows_here, :].astype(jnp.float32)
                total = total + recv[1][rows_here, :].astype(jnp.float32)
            elif has_recv:
                total = total + recv[n][rows_here, :].astype(jnp.float32)
            out[rows_here, :] = total.astype(out.dtype)

    for n, (d, valid, place) in enumerate(jobs):
        if valid is None:
            fetch(n, d, place)
        else:
            pl.when(valid)(functools.partial(fetch, n, d, place))
    for n, (d, valid, place) in enumerate(jobs):
        if valid is None:
            multiply(n, outs[n])
        else:
            pl.when(valid)(functools.partial(multiply, n, outs[n]))


def hop(t, size, where, blocks, own, held, recv):
    wide = own is not None
    slots = () if wide else tuple(slots_at(t, size))
    rows = own.shape[0] // size if wide else held[0][0].shape[0]
    cells = sum(group[0].shape[0] for group in blocks)
    width = blocks[0][0].shape[1]
    count = 1 if t == size else 2
    kept = jnp.float32 if t == size and recv is None else jnp.bfloat16
    spec = pl.BlockSpec(memory_space=pltpu.VMEM)
    any_spec = pl.BlockSpec(memory_space=HBM)
    shards = [own] if wide else [shard for j in slots for shard in held[j]]
    operands = [where, *[block for group in blocks for block in group], *shards, *(recv or [])]
    in_specs = [pl.BlockSpec(memory_space=SMEM)] + [spec] * (4 * len(blocks)) + [any_spec] * len(shards)
    in_specs += [spec] * len(recv or [])
    return pl.pallas_call(
        functools.partial(hop_kernel, t, size, wide, slots, len(blocks), recv is not None),
        out_shape=[jax.ShapeDtypeStruct((cells, rows), kept)] * count,
        in_specs=in_specs,
        out_specs=[spec] * count,
        scratch_shapes=[
            pltpu.VMEM((count, rows, 4 * width), jnp.bfloat16),
            pltpu.SemaphoreType.DMA((count,)),
        ],
        compiler_params=pltpu.CompilerParams(vmem_limit_bytes=HOP_LIMIT),
        cost_estimate=takes(2 + cells / 300),
    )(*operands)


def on_device(deviation, courant, collide, hole_cells, hole_wall, specular, specularity):
    n_space, n_row, n_col = (lax.axis_size(name) for name in ("space", "mrow", "mcol"))
    s, r, c = (lax.axis_index(name) for name in ("space", "mrow", "mcol"))
    width_x, width_y, block_len = deviation.shape
    cell_count = width_x * width_y
    slot_count = hole_cells.shape[0]
    wall_count, mode_count = specular.shape
    piece = block_len // (n_row * n_col)
    groups = n_row * n_col
    vmem = pl.BlockSpec()
    hbm = pl.BlockSpec(memory_space=HBM)
    smem = pl.BlockSpec(memory_space=SMEM)
    params = pltpu.CompilerParams(vmem_limit_bytes=LIMIT)
    where = jnp.stack([s, r, c]).astype(jnp.int32)

    up = [(i, i + 1) for i in range(n_space - 1)]
    down = [(j, i) for i, j in up]
    before_layer = lax.ppermute(deviation[-1:], "space", up)
    after_layer = lax.ppermute(deviation[:1], "space", down)

    def after(value, *first):
        return lax.optimization_barrier((value, first))[0]

    def shape(*dims):
        return jax.ShapeDtypeStruct(dims, jnp.bfloat16)

    head = cell_count - slot_count
    sizes = [head * part // sum(SPLIT) for part in SPLIT]
    count = len(sizes)
    lane_cells = hole_cells[None, :]
    wide = n_space != 2
    rows = collide.shape[0] // n_col
    own = lax.all_gather(collide, "space", axis=1, tiled=True) if wide else None
    shards = 0 if wide else n_col - 1
    swap = [(0, 1), (1, 0)]
    held, order, first = [], jnp.asarray(line_steps(n_col)), ()
    if not wide:
        first = pl.pallas_call(
            pick_kernel,
            out_shape=shape(rows, collide.shape[1]),
            in_specs=[smem, smem, hbm],
            out_specs=vmem,
            scratch_shapes=[pltpu.SemaphoreType.DMA],
            compiler_params=params,
            cost_estimate=takes(2),
        )(where, order, collide)
        held.append((first, lax.ppermute(after(first, before_layer, after_layer), "space", swap)))
    payload, extra, *mine = pl.pallas_call(
        functools.partial(read_kernel, n_row, n_col, count, shards),
        out_shape=[shape(groups, piece + TAIL, slot_count), shape(slot_count, block_len)]
        + [shape(size, block_len) for size in sizes]
        + [shape(rows, collide.shape[1])] * shards,
        in_specs=[vmem] * 5 + [smem, smem, hbm][: shards * 3],
        out_specs=[vmem] * (count + 2) + [hbm] * shards,
        scratch_shapes=[
            pltpu.VMEM((cell_count, block_len), jnp.bfloat16),
            pltpu.VMEM((slot_count, cell_count), jnp.bfloat16),
            pltpu.VMEM((head, slot_count), jnp.bfloat16),
            pltpu.VMEM((slot_count, slot_count), jnp.bfloat16),
            pltpu.VMEM((head, 1), jnp.float32),
        ]
        + [
            pltpu.VMEM((shards, rows, collide.shape[1]), jnp.bfloat16),
            pltpu.SemaphoreType.DMA((shards,)),
            pltpu.SemaphoreType.DMA((shards,)),
        ][: shards * 3],
        compiler_params=params,
        cost_estimate=takes(7),
    )(
        deviation,
        before_layer,
        after_layer,
        courant,
        after(lane_cells, first),
        *([] if wide else [where, order, collide]),
    )
    mine, parts = mine[:count], mine[count:]
    for part in parts:
        held.append((part, lax.ppermute(part, "space", swap)))

    flip = [[(i, i ^ bit) for i in range(n_row)] for bit in (1, 2)]
    right = [(i, i + 1) for i in range(n_col - 1)]
    left = [(j, i) for i, j in right]
    far = []
    for value in mine:
        far.append(lax.ppermute(value, "mrow", flip[1]))
    arrived = lax.all_to_all(payload, ("mrow", "mcol"), split_axis=0, concat_axis=0, tiled=True)
    def send(t, value):
        return [
            lax.ppermute(value[0], "mcol", right[:t]),
            lax.ppermute(value[1], "mcol", left[n_col - 1 - t :]),
        ]

    state = {}
    done = ()

    def step(t, n, *ready):
        return hop(t, n_col, after(where, *done, *ready), chunks[n], own, held, state.get(n))

    def gather(n):
        near = lax.ppermute(mine[n], "mrow", flip[0])
        both = lax.ppermute(after(far[n], *done), "mrow", flip[0])
        return [mine[n], near, far[n], both]

    own_table = lax.dynamic_slice_in_dim(specular, (c * n_row + r) * block_len, block_len, 1)
    mirror, place, fill, spare, on_rim = pl.pallas_call(
        functools.partial(late_mask_kernel, n_row, n_col),
        out_shape=[
            shape(wall_count, block_len, block_len),
            shape(cell_count, slot_count),
            shape(head, slot_count),
            shape(slot_count, slot_count),
            jax.ShapeDtypeStruct((head, 1), jnp.float32),
        ],
        in_specs=[vmem] * 2,
        out_specs=[vmem] * 5,
        compiler_params=params,
        cost_estimate=takes(4),
    )(after(lane_cells, extra), own_table)
    far[0] = after(far[0], mirror)
    chunks = [[gather(0)]]
    done = step(1, 0)
    state[0] = send(1, done)
    mine.append(
        pl.pallas_call(
            functools.partial(rim_kernel, mode_count),
            out_shape=shape(slot_count, block_len),
            in_specs=[smem] + [vmem] * 5,
            out_specs=vmem,
            compiler_params=params,
            cost_estimate=takes(4),
        )(specularity, after(arrived, *done), mirror, hole_wall[None, :], lane_cells, extra)
    )
    far.append(lax.ppermute(mine[count], "mrow", flip[1]))
    chunks.append([gather(n) for n in range(1, count + 1)])
    done = step(1, 1, *state[0])
    state[1] = send(1, done)
    outs = []
    for t in range(2, n_col + 1):
        for n in (0, 1):
            if (t, n) == (n_col, 1):
                continue
            done = step(t, n)
            if t == n_col:
                outs.append(done[0])
            else:
                state[n] = send(t, done)
    total = hop(n_col, n_col, after(where, *done), chunks[1], own, held, None)[0]
    ends = pl.pallas_call(
        ends_kernel,
        out_shape=jax.ShapeDtypeStruct((slot_count, rows), jnp.float32),
        in_specs=[vmem] * (1 + len(outs)),
        out_specs=vmem,
        compiler_params=params,
        cost_estimate=takes(2),
    )(fill, *outs)
    out = pl.pallas_call(
        merge_kernel,
        out_shape=shape(cell_count, rows),
        in_specs=[vmem] * (8 + len(outs)),
        out_specs=vmem,
        compiler_params=params,
        cost_estimate=takes(4),
    )(fill, spare, place, on_rim, ends, total, *state[1], *outs)
    return out.reshape(width_x, width_y, rows)


def solution(mesh):
    in_specs = (
        P("space", None, ("mcol", "mrow")),
        P(None, ("mcol", "mrow")),
        P("mrow", ("mcol", "space")),
        P("space"),
        P("space"),
        P(),
        P(),
    )
    out_specs = P("space", None, ("mrow", "mcol"))
    return jax.shard_map(
        on_device, mesh=mesh, in_specs=in_specs, out_specs=out_specs, check_vma=False
    )
```

```python
import functools
import jax
import jax.numpy as jnp
import numpy as np
from jax import lax
from jax.experimental import pallas as pl
from jax.experimental.pallas import tpu as pltpu
from jax.sharding import PartitionSpec as P

SMEM = pltpu.SMEM
HBM = pltpu.HBM
NT = (((1,), (1,)), ((), ()))
SPLIT = (2, 1)
LIMIT = 60 * 1024 * 1024
HOP_LIMIT = 16 * 1024 * 1024


def takes(microseconds):
    return pl.CostEstimate(flops=int(microseconds * 0.5e9), bytes_accessed=0, transcendentals=0)


TAIL = 16


def line_steps(size):
    order = []
    for c in range(size):
        row = []
        for t in range(1, size):
            if c <= t - 1:
                row.append(c + size - t)
            if c >= size - t:
                row.append(c - size + t)
        row.append(c)
        order.append(row)
    return np.array(order, np.int32)


def slot_of(c, t, size):
    place = 0
    for u in range(1, t):
        place = place + jnp.where(c <= u - 1, 1, 0) + jnp.where(c >= size - u, 1, 0)
    return place


def slots_at(t, size):
    found = set()
    for c in range(size):
        place = 0
        for u in range(1, size):
            for hit in (c <= u - 1, c >= size - u):
                if hit:
                    if u == t:
                        found.add(place)
                    place += 1
        if t == size:
            found.add(size - 1)
    return sorted(found)


def moves(lane, head, fill, spare, on_rim):
    slots = lane.shape[1]
    sub = jnp.broadcast_to(lane, (128, slots)).T[:, 0:1]
    total = jnp.sum((lane >= 0).astype(jnp.float32), axis=1, keepdims=True).astype(jnp.int32)
    in_head = jnp.logical_and(lane >= 0, lane < head)
    head_count = jnp.sum(in_head.astype(jnp.float32), axis=1, keepdims=True).astype(jnp.int32)
    place = lax.broadcasted_iota(jnp.int32, (1, slots), 1)
    tail = jnp.broadcast_to(place + head, (slots, slots))
    wide_sub = jnp.broadcast_to(sub, (slots, slots))
    before = jnp.logical_and(wide_sub >= head, wide_sub < tail).astype(jnp.float32)
    hit = (wide_sub == tail).astype(jnp.float32)
    rank = place - jnp.sum(before, axis=0, keepdims=True).astype(jnp.int32)
    tail_key = jnp.where(jnp.sum(hit, axis=0, keepdims=True) > 0, -2, rank)
    row = lax.broadcasted_iota(jnp.int32, (head, slots), 0)
    wide_lane = jnp.broadcast_to(lane, (head, slots))
    ahead = jnp.logical_and(wide_lane >= 0, wide_lane < row).astype(jnp.float32)
    hits = jnp.max((wide_lane == row).astype(jnp.float32), axis=1, keepdims=True)
    head_key = jnp.where(hits > 0, jnp.sum(ahead, axis=1, keepdims=True).astype(jnp.int32), -1)
    on_rim[...] = hits
    fill[...] = (head_key == tail_key).astype(jnp.float32).astype(jnp.bfloat16)
    slot = lax.broadcasted_iota(jnp.int32, (slots, 1), 0)
    slot_key = jnp.where(slot >= total, slot - total + head_count, -1)
    spare[...] = (slot_key == tail_key).astype(jnp.float32).astype(jnp.bfloat16)
    return sub


def late_mask_kernel(rows_of, cols_of, cells_lane, table, mirror, place, fill, spare, on_rim):
    cell = lax.broadcasted_iota(jnp.int32, place.shape, 0)
    place[...] = (cells_lane[...] == cell).astype(jnp.float32).astype(jnp.bfloat16)
    modes = mirror.shape[1]
    piece = modes // (rows_of * cols_of)
    entry = table[...]
    block = lax.div(entry, modes)
    group = lax.rem(block, rows_of) * cols_of + lax.div(block, rows_of)
    position = group * piece + lax.rem(entry, piece)
    source = lax.broadcasted_iota(jnp.int32, mirror.shape[1:], 0)
    for w in range(mirror.shape[0]):
        mirror[w] = (position[w : w + 1] == source).astype(jnp.float32).astype(jnp.bfloat16)
    moves(cells_lane[...], fill.shape[0], fill, spare, on_rim)


def read_kernel(rows_of, cols_of, count, shards, *refs):
    refs = list(refs)
    dev, before, after, courant, cells_lane = (refs.pop(0) for _ in range(5))
    where, table, whole = (refs.pop(0) for _ in range(3)) if shards else (None, None, None)
    payload, extra = refs.pop(0), refs.pop(0)
    outs = [refs.pop(0) for _ in range(count)]
    parts = [refs.pop(0) for _ in range(shards)]
    read, select, fill, spare, on_rim = (refs.pop(0) for _ in range(5))
    fetches, stores = [], []
    if shards:
        stage, in_sem, out_sem = refs
        rows = stage.shape[1]
        for j in range(shards):
            first = pl.multiple_of(table[where[2], j] * rows, rows)
            fetches.append(
                pltpu.make_async_copy(whole.at[pl.ds(first, rows), :], stage.at[j], in_sem.at[j])
            )
            stores.append(pltpu.make_async_copy(stage.at[j], parts[j], out_sem.at[j]))
    for copy in fetches:
        copy.start()
    sub = moves(cells_lane[...], fill.shape[0], fill, spare, on_rim)
    cell = lax.broadcasted_iota(jnp.int32, select.shape, 1)
    select[...] = (sub == cell).astype(jnp.float32).astype(jnp.bfloat16)
    width_x, width_y, modes = dev.shape
    speed = courant[...]
    reach = jnp.abs(speed)
    ahead = speed > 0
    a = jnp.broadcast_to(reach[0:1], (width_y, modes))
    b = jnp.broadcast_to(reach[1:2], (width_y, modes))
    ahead_x = jnp.broadcast_to(ahead[0:1], (width_y, modes))
    ahead_y = jnp.broadcast_to(ahead[1:2], (width_y, modes))

    def one(x, low, high):
        center = dev[x].astype(jnp.float32)
        ux = jnp.where(ahead_x, low.astype(jnp.float32), high.astype(jnp.float32))
        along = (1.0 - a) * center + a * ux
        shifted = jnp.where(ahead_y, pltpu.roll(along, 1, 0), pltpu.roll(along, width_y - 1, 0))
        read[pl.ds(pl.multiple_of(x * width_y, 16), width_y), :] = (
            (1.0 - b) * along + b * shifted
        ).astype(read.dtype)

    one(0, before[0], dev[1])

    def body(x, carry):
        one(x, dev[x - 1], dev[x + 1])
        return carry

    lax.fori_loop(1, width_x - 1, body, 0)
    one(width_x - 1, dev[width_x - 2], after[0])

    for fetch, store in zip(fetches, stores):
        fetch.wait()
        store.start()
    head = read.shape[0] - extra.shape[0]
    tail_rows = read[head:, :]
    first = 0
    for out in outs:
        rows = slice(first, first + out.shape[0])
        first += out.shape[0]
        moved = jnp.dot(fill[rows, :], tail_rows, preferred_element_type=jnp.float32)
        kept = read[rows, :].astype(jnp.float32)
        out[...] = jnp.where(on_rim[rows, :] > 0, moved, kept).astype(out.dtype)
    extra[...] = jnp.dot(spare[...], tail_rows, preferred_element_type=jnp.float32).astype(extra.dtype)

    rim = jnp.dot(select[...], read[...], preferred_element_type=jnp.float32)
    flipped = rim.T
    total = jnp.sum(flipped, axis=0, keepdims=True)
    high = total.astype(jnp.bfloat16).astype(jnp.float32)
    middle = (total - high).astype(jnp.bfloat16).astype(jnp.float32)
    low = total - high - middle
    place = lax.broadcasted_iota(jnp.int32, (TAIL, total.shape[1]), 0)
    tail = jnp.where(place == 0, high, jnp.where(place == 1, middle, jnp.where(place == 2, low, 0.0)))
    tail = tail.astype(jnp.bfloat16)
    piece = modes // (rows_of * cols_of)
    packed = flipped.astype(jnp.bfloat16)
    for r in range(rows_of):
        for c in range(cols_of):
            block = c * rows_of + r
            payload[r * cols_of + c, 0:piece, :] = packed[block * piece : (block + 1) * piece]
            payload[r * cols_of + c, piece : piece + TAIL, :] = tail
    for store in stores:
        store.wait()


def rim_kernel(mode_count, specularity, arrived, mirror, wall, cells_lane, extra, out):
    groups, height, slots = arrived.shape
    piece = height - TAIL
    values = arrived[:, 0:piece, :].reshape(groups * piece, slots).T
    sums = arrived[:, piece:height, :].reshape(groups * TAIL, slots).astype(jnp.float32)
    total = jnp.broadcast_to(jnp.sum(sums, axis=0, keepdims=True), (128, slots)).T
    diffuse = total[:, 0:1] / mode_count
    walls = jnp.broadcast_to(wall[...], (128, slots)).T[:, 0:1]
    share = jnp.zeros(walls.shape, jnp.float32)
    mirrored = jnp.zeros(out.shape, jnp.float32)
    for w in range(mirror.shape[0]):
        share = jnp.where(walls == w, specularity[w], share)
        picked = jnp.dot(values, mirror[w], preferred_element_type=jnp.float32)
        mirrored = jnp.where(walls == w, picked, mirrored)
    emitted = share * mirrored + (1.0 - share) * diffuse
    used = jnp.broadcast_to(cells_lane[...], (128, slots)).T[:, 0:1] >= 0
    out[...] = jnp.where(used, emitted, extra[...].astype(jnp.float32)).astype(out.dtype)


def base_kernel(fill, on_rim, part, base):
    kept = part.shape[0]
    base[:kept, :] = jnp.where(on_rim[...] > 0, 0.0, part[...].astype(jnp.float32)).astype(base.dtype)
    moved = lax.dot_general(
        fill[...], part[...], (((0,), (0,)), ((), ())), preferred_element_type=jnp.float32
    )
    base[kept:, :] = moved.astype(base.dtype)


def merge_kernel(fill, spare, place, on_rim, base, total, from_left, from_right, out):
    slots = spare.shape[0]
    kept = base.shape[0] - slots
    total = total[...] + from_left[...].astype(jnp.float32) + from_right[...].astype(jnp.float32)
    total = total.astype(jnp.bfloat16)
    more = total.shape[0] - slots
    part, last = total[:more, :], total[more:, :]
    head = kept + more
    tn = (((0,), (0,)), ((), ()))
    moved = jnp.dot(place[:kept, :], last, preferred_element_type=jnp.float32)
    out[:kept, :] = (base[:kept, :].astype(jnp.float32) + moved).astype(out.dtype)
    moved = jnp.dot(place[kept:head, :], last, preferred_element_type=jnp.float32)
    out[kept:head, :] = jnp.where(on_rim[...] > 0, moved, part.astype(jnp.float32)).astype(out.dtype)
    moved = jnp.dot(place[head:, :], last, preferred_element_type=jnp.float32)
    moved = moved + lax.dot_general(spare[...], last, tn, preferred_element_type=jnp.float32)
    moved = moved + lax.dot_general(fill[...], part, tn, preferred_element_type=jnp.float32)
    out[head:, :] = (base[kept:, :].astype(jnp.float32) + moved).astype(out.dtype)


def hop_kernel(t, size, wide, slots, groups, has_recv, *refs):
    refs = list(refs)
    where = refs.pop(0)
    blocks = [[refs.pop(0) for _ in range(4)] for _ in range(groups)]
    own = refs.pop(0) if wide else None
    held = {j: (refs.pop(0), refs.pop(0)) for j in slots}
    final = t == size
    recv = [refs.pop(0), refs.pop(0)] if has_recv else None
    outs = [refs.pop(0)] if final else [refs.pop(0), refs.pop(0)]
    buffer, sem = refs
    s, r, c = where[0], where[1], where[2]
    rows = buffer.shape[1]
    width = blocks[0][0].shape[1]
    if final:
        jobs = [(c, None, size - 1)]
    else:
        first = slot_of(c, t, size)
        goes_right = c <= t - 1
        jobs = [
            (c + size - t, goes_right, first),
            (c - size + t, c >= size - t, first + jnp.where(goes_right, 1, 0)),
        ]

    def fetch(n, d, place):
        for b in range(4):
            source = lax.bitwise_xor(r, b)
            target = buffer.at[n, :, b * width : (b + 1) * width]
            if wide:
                column = pl.multiple_of(source * width, width)
                pltpu.make_async_copy(
                    own.at[pl.ds(pl.multiple_of(d * rows, rows), rows), pl.ds(column, width)],
                    target,
                    sem.at[n],
                ).start()
                continue
            column = pl.multiple_of(lax.bitwise_and(source, 1) * width, width)
            is_own = lax.shift_right_logical(source, 1) == s
            for j, pair in held.items():
                for use, shard in ((is_own, pair[0]), (jnp.logical_not(is_own), pair[1])):

                    @pl.when(jnp.logical_and(use, place == j))
                    def _(shard=shard):
                        pltpu.make_async_copy(shard.at[:, pl.ds(column, width)], target, sem.at[n]).start()

    def multiply(n, out):
        pltpu.make_async_copy(buffer.at[n], buffer.at[n], sem.at[n]).wait()
        first = 0
        for group in blocks:
            rows_here = slice(first, first + group[0].shape[0])
            first += group[0].shape[0]
            total = None
            for b in range(4):
                part = lax.dot_general(
                    group[b][...],
                    buffer[n, :, b * width : (b + 1) * width],
                    NT,
                    preferred_element_type=jnp.float32,
                )
                total = part if total is None else total + part
            if final and has_recv:
                total = total + recv[0][rows_here, :].astype(jnp.float32)
                total = total + recv[1][rows_here, :].astype(jnp.float32)
            elif has_recv:
                total = total + recv[n][rows_here, :].astype(jnp.float32)
            out[rows_here, :] = total.astype(out.dtype)

    for n, (d, valid, place) in enumerate(jobs):
        if valid is None:
            fetch(n, d, place)
        else:
            pl.when(valid)(functools.partial(fetch, n, d, place))
    for n, (d, valid, place) in enumerate(jobs):
        if valid is None:
            multiply(n, outs[n])
        else:
            pl.when(valid)(functools.partial(multiply, n, outs[n]))


def hop(t, size, where, blocks, own, held, recv):
    wide = own is not None
    slots = () if wide else tuple(slots_at(t, size))
    rows = own.shape[0] // size if wide else held[0][0].shape[0]
    cells = sum(group[0].shape[0] for group in blocks)
    width = blocks[0][0].shape[1]
    count = 1 if t == size else 2
    kept = jnp.float32 if t == size and recv is None else jnp.bfloat16
    spec = pl.BlockSpec(memory_space=pltpu.VMEM)
    any_spec = pl.BlockSpec(memory_space=HBM)
    shards = [own] if wide else [shard for j in slots for shard in held[j]]
    operands = [where, *[block for group in blocks for block in group], *shards, *(recv or [])]
    in_specs = [pl.BlockSpec(memory_space=SMEM)] + [spec] * (4 * len(blocks)) + [any_spec] * len(shards)
    in_specs += [spec] * len(recv or [])
    return pl.pallas_call(
        functools.partial(hop_kernel, t, size, wide, slots, len(blocks), recv is not None),
        out_shape=[jax.ShapeDtypeStruct((cells, rows), kept)] * count,
        in_specs=in_specs,
        out_specs=[spec] * count,
        scratch_shapes=[
            pltpu.VMEM((count, rows, 4 * width), jnp.bfloat16),
            pltpu.SemaphoreType.DMA((count,)),
        ],
        compiler_params=pltpu.CompilerParams(vmem_limit_bytes=HOP_LIMIT),
        cost_estimate=takes(2 + cells / 300),
    )(*operands)


def on_device(deviation, courant, collide, hole_cells, hole_wall, specular, specularity):
    n_space, n_row, n_col = (lax.axis_size(name) for name in ("space", "mrow", "mcol"))
    s, r, c = (lax.axis_index(name) for name in ("space", "mrow", "mcol"))
    width_x, width_y, block_len = deviation.shape
    cell_count = width_x * width_y
    slot_count = hole_cells.shape[0]
    wall_count, mode_count = specular.shape
    piece = block_len // (n_row * n_col)
    groups = n_row * n_col
    vmem = pl.BlockSpec()
    hbm = pl.BlockSpec(memory_space=HBM)
    smem = pl.BlockSpec(memory_space=SMEM)
    params = pltpu.CompilerParams(vmem_limit_bytes=LIMIT)
    where = jnp.stack([s, r, c]).astype(jnp.int32)

    if n_space == 2:
        edge = jnp.where(s == 0, deviation[-1:], deviation[:1])
        edge = lax.ppermute(edge, "space", [(0, 1), (1, 0)])
        none = jnp.zeros_like(edge)
        before_layer, after_layer = jnp.where(s == 1, edge, none), jnp.where(s == 0, edge, none)
    else:
        up = [(i, i + 1) for i in range(n_space - 1)]
        down = [(j, i) for i, j in up]
        before_layer = lax.ppermute(deviation[-1:], "space", up)
        after_layer = lax.ppermute(deviation[:1], "space", down)

    def after(value, *first):
        return lax.optimization_barrier((value, first))[0]

    def shape(*dims):
        return jax.ShapeDtypeStruct(dims, jnp.bfloat16)

    head = cell_count - slot_count
    sizes = [head * part // sum(SPLIT) for part in SPLIT]
    count = len(sizes)
    lane_cells = hole_cells[None, :]
    wide = n_space != 2
    rows = collide.shape[0] // n_col
    own = lax.all_gather(collide, "space", axis=1, tiled=True) if wide else None
    shards = 0 if wide else n_col
    swap = [(0, 1), (1, 0)]
    held, order = [], jnp.asarray(line_steps(n_col))
    payload, extra, *mine = pl.pallas_call(
        functools.partial(read_kernel, n_row, n_col, count, shards),
        out_shape=[shape(groups, piece + TAIL, slot_count), shape(slot_count, block_len)]
        + [shape(size, block_len) for size in sizes]
        + [shape(rows, collide.shape[1])] * shards,
        in_specs=[vmem] * 5 + [smem, smem, hbm][: shards * 3],
        out_specs=[vmem] * (count + 2) + [hbm] * shards,
        scratch_shapes=[
            pltpu.VMEM((cell_count, block_len), jnp.bfloat16),
            pltpu.VMEM((slot_count, cell_count), jnp.bfloat16),
            pltpu.VMEM((head, slot_count), jnp.bfloat16),
            pltpu.VMEM((slot_count, slot_count), jnp.bfloat16),
            pltpu.VMEM((head, 1), jnp.float32),
        ]
        + [
            pltpu.VMEM((shards, rows, collide.shape[1]), jnp.bfloat16),
            pltpu.SemaphoreType.DMA((shards,)),
            pltpu.SemaphoreType.DMA((shards,)),
        ][: shards * 3],
        compiler_params=params,
        cost_estimate=takes(7),
    )(
        deviation,
        before_layer,
        after_layer,
        courant,
        lane_cells,
        *([] if wide else [where, order, collide]),
    )
    mine, parts = mine[:count], mine[count:]
    for part in parts:
        held.append((part, lax.ppermute(part, "space", swap)))

    flip = [[(i, i ^ bit) for i in range(n_row)] for bit in (1, 2)]
    right = [(i, i + 1) for i in range(n_col - 1)]
    left = [(j, i) for i, j in right]
    far = []
    for value in mine:
        far.append(lax.ppermute(value, "mrow", flip[1]))
    arrived = lax.all_to_all(payload, ("mrow", "mcol"), split_axis=0, concat_axis=0, tiled=True)
    def send(t, value):
        return [
            lax.ppermute(value[0], "mcol", right[:t]),
            lax.ppermute(value[1], "mcol", left[n_col - 1 - t :]),
        ]

    state = {}
    done = ()

    def step(t, n, *ready):
        return hop(t, n_col, after(where, *done, *ready), chunks[n], own, held, state.get(n))

    def gather(n):
        near = lax.ppermute(mine[n], "mrow", flip[0])
        both = lax.ppermute(after(far[n], *done), "mrow", flip[0])
        return [mine[n], near, far[n], both]

    own_table = lax.dynamic_slice_in_dim(specular, (c * n_row + r) * block_len, block_len, 1)
    mirror, place, fill, spare, on_rim = pl.pallas_call(
        functools.partial(late_mask_kernel, n_row, n_col),
        out_shape=[
            shape(wall_count, block_len, block_len),
            shape(cell_count, slot_count),
            shape(head, slot_count),
            shape(slot_count, slot_count),
            jax.ShapeDtypeStruct((head, 1), jnp.float32),
        ],
        in_specs=[vmem] * 2,
        out_specs=[vmem] * 5,
        compiler_params=params,
        cost_estimate=takes(4),
    )(after(lane_cells, extra), own_table)
    far[0] = after(far[0], mirror, *[other for _, other in held[:1]])
    chunks = [[gather(0)]]
    done = step(1, 0, arrived)
    state[0] = send(1, done)
    mine.append(
        pl.pallas_call(
            functools.partial(rim_kernel, mode_count),
            out_shape=shape(slot_count, block_len),
            in_specs=[smem] + [vmem] * 5,
            out_specs=vmem,
            compiler_params=params,
            cost_estimate=takes(4),
        )(specularity, after(arrived, far[1], *done), mirror, hole_wall[None, :], lane_cells, extra)
    )
    far.append(lax.ppermute(mine[count], "mrow", flip[1]))
    chunks.append([gather(n) for n in range(1, count + 1)])
    done = step(1, 1, *state[0])
    state[1] = send(1, done)
    outs = []
    for t in range(2, n_col + 1):
        for n in (0, 1):
            if (t, n) == (n_col, 1):
                continue
            done = step(t, n)
            if t == n_col:
                outs.append(done[0])
            else:
                state[n] = send(t, done)
    total = hop(n_col, n_col, after(where, *done), chunks[1], own, held, None)[0]
    base = pl.pallas_call(
        base_kernel,
        out_shape=shape(sizes[0] + slot_count, rows),
        grid=(1,),
        in_specs=[
            pl.BlockSpec((sizes[0], slot_count), lambda i: (0, 0)),
            pl.BlockSpec((sizes[0], 1), lambda i: (0, 0)),
            pl.BlockSpec((sizes[0], rows), lambda i: (0, 0)),
        ],
        out_specs=pl.BlockSpec((sizes[0] + slot_count, rows), lambda i: (0, 0)),
        compiler_params=params,
        cost_estimate=takes(2),
    )(fill, on_rim, *outs)
    near = pl.BlockSpec(memory_space=pltpu.VMEM)
    out = pl.pallas_call(
        merge_kernel,
        out_shape=shape(cell_count, rows),
        in_specs=[near] * 8,
        out_specs=vmem,
        compiler_params=pltpu.CompilerParams(vmem_limit_bytes=HOP_LIMIT),
        cost_estimate=takes(4),
    )(fill[sizes[0] :], spare, place, on_rim[sizes[0] :], base, total, *state[1])
    return out.reshape(width_x, width_y, rows)


def solution(mesh):
    in_specs = (
        P("space", None, ("mcol", "mrow")),
        P(None, ("mcol", "mrow")),
        P("mrow", ("mcol", "space")),
        P("space"),
        P("space"),
        P(),
        P(),
    )
    out_specs = P("space", None, ("mrow", "mcol"))
    return jax.shard_map(
        on_device, mesh=mesh, in_specs=in_specs, out_specs=out_specs, check_vma=False
    )
```

```python
import functools
import jax
import jax.numpy as jnp
import numpy as np
from jax import lax
from jax.experimental import pallas as pl
from jax.experimental.pallas import tpu as pltpu
from jax.sharding import PartitionSpec as P

SMEM = pltpu.SMEM
HBM = pltpu.HBM
NT = (((1,), (1,)), ((), ()))
SPLIT = (2, 1)
LIMIT = 60 * 1024 * 1024
HOP_LIMIT = 16 * 1024 * 1024


def takes(microseconds):
    return pl.CostEstimate(flops=int(microseconds * 0.5e9), bytes_accessed=0, transcendentals=0)


TAIL = 16


def line_steps(size):
    order = []
    for c in range(size):
        row = []
        for t in range(1, size):
            if c <= t - 1:
                row.append(c + size - t)
            if c >= size - t:
                row.append(c - size + t)
        row.append(c)
        order.append(row)
    return np.array(order, np.int32)


def slot_of(c, t, size):
    place = 0
    for u in range(1, t):
        place = place + jnp.where(c <= u - 1, 1, 0) + jnp.where(c >= size - u, 1, 0)
    return place


def slots_at(t, size):
    found = set()
    for c in range(size):
        place = 0
        for u in range(1, size):
            for hit in (c <= u - 1, c >= size - u):
                if hit:
                    if u == t:
                        found.add(place)
                    place += 1
        if t == size:
            found.add(size - 1)
    return sorted(found)


def moves(lane, head, fill, spare, on_rim):
    slots = lane.shape[1]
    sub = jnp.broadcast_to(lane, (128, slots)).T[:, 0:1]
    total = jnp.sum((lane >= 0).astype(jnp.float32), axis=1, keepdims=True).astype(jnp.int32)
    in_head = jnp.logical_and(lane >= 0, lane < head)
    head_count = jnp.sum(in_head.astype(jnp.float32), axis=1, keepdims=True).astype(jnp.int32)
    place = lax.broadcasted_iota(jnp.int32, (1, slots), 1)
    tail = jnp.broadcast_to(place + head, (slots, slots))
    wide_sub = jnp.broadcast_to(sub, (slots, slots))
    before = jnp.logical_and(wide_sub >= head, wide_sub < tail).astype(jnp.float32)
    hit = (wide_sub == tail).astype(jnp.float32)
    rank = place - jnp.sum(before, axis=0, keepdims=True).astype(jnp.int32)
    tail_key = jnp.where(jnp.sum(hit, axis=0, keepdims=True) > 0, -2, rank)
    row = lax.broadcasted_iota(jnp.int32, (head, slots), 0)
    wide_lane = jnp.broadcast_to(lane, (head, slots))
    ahead = jnp.logical_and(wide_lane >= 0, wide_lane < row).astype(jnp.float32)
    hits = jnp.max((wide_lane == row).astype(jnp.float32), axis=1, keepdims=True)
    head_key = jnp.where(hits > 0, jnp.sum(ahead, axis=1, keepdims=True).astype(jnp.int32), -1)
    on_rim[...] = hits
    fill[...] = (head_key == tail_key).astype(jnp.float32).astype(jnp.bfloat16)
    slot = lax.broadcasted_iota(jnp.int32, (slots, 1), 0)
    slot_key = jnp.where(slot >= total, slot - total + head_count, -1)
    spare[...] = (slot_key == tail_key).astype(jnp.float32).astype(jnp.bfloat16)
    return sub


def late_mask_kernel(
    rows_of, cols_of, cells_lane, table, mirror, place, spare, fill, fill_more, on_rim, on_rim_more, fills, flags
):
    cell = lax.broadcasted_iota(jnp.int32, place.shape, 0)
    place[...] = (cells_lane[...] == cell).astype(jnp.float32).astype(jnp.bfloat16)
    modes = mirror.shape[1]
    piece = modes // (rows_of * cols_of)
    entry = table[...]
    block = lax.div(entry, modes)
    group = lax.rem(block, rows_of) * cols_of + lax.div(block, rows_of)
    position = group * piece + lax.rem(entry, piece)
    source = lax.broadcasted_iota(jnp.int32, mirror.shape[1:], 0)
    for w in range(mirror.shape[0]):
        mirror[w] = (position[w : w + 1] == source).astype(jnp.float32).astype(jnp.bfloat16)
    moves(cells_lane[...], fills.shape[0], fills, spare, flags)
    kept = fill.shape[0]
    fill[...] = fills[:kept, :]
    fill_more[...] = fills[kept:, :]
    on_rim[...] = flags[:kept, :]
    on_rim_more[...] = flags[kept:, :]


def read_kernel(count, shards, *refs):
    refs = list(refs)
    where, dev, courant, cells_lane = (refs.pop(0) for _ in range(4))
    edges = [refs.pop(0) for _ in range(2 if not shards else 1)]
    table, whole = (refs.pop(0) for _ in range(2)) if shards else (None, None)
    extra = refs.pop(0)
    outs = [refs.pop(0) for _ in range(count)]
    parts = [refs.pop(0) for _ in range(shards)]
    read, fill, spare, on_rim = (refs.pop(0) for _ in range(4))
    fetches, stores = [], []
    if shards:
        stage, in_sem, out_sem = refs
        rows = stage.shape[1]
        for j in range(shards):
            first = pl.multiple_of(table[where[2], j] * rows, rows)
            fetches.append(
                pltpu.make_async_copy(whole.at[pl.ds(first, rows), :], stage.at[j], in_sem.at[j])
            )
            stores.append(pltpu.make_async_copy(stage.at[j], parts[j], out_sem.at[j]))
    for copy in fetches:
        copy.start()
    moves(cells_lane[...], fill.shape[0], fill, spare, on_rim)
    width_x, width_y, modes = dev.shape
    speed = courant[...]
    reach = jnp.abs(speed)
    ahead = jnp.where(speed > 0, 1.0, 0.0)
    if shards:
        edge = edges[0][0].astype(jnp.float32)
        before, after = jnp.where(where[0] == 1, edge, 0.0), jnp.where(where[0] == 0, edge, 0.0)
    else:
        before, after = edges[0][0].astype(jnp.float32), edges[1][0].astype(jnp.float32)
    lanes = 128
    moving = list(zip(fetches, stores))
    for low in range(0, modes, lanes):
        if low and moving:
            fetch, store = moving.pop(0)
            fetch.wait()
            store.start()
        cut = slice(low, low + lanes)
        a, b = reach[0:1, cut], reach[1:2, cut]
        stay_x, stay_y = 1.0 - a, 1.0 - b
        ahead_x = jnp.broadcast_to(ahead[0:1, cut], (width_y, lanes)) > 0
        ahead_y = jnp.broadcast_to(ahead[1:2, cut], (width_y, lanes)) > 0

        def one(x, behind, center, beyond):
            along = stay_x * center + a * jnp.where(ahead_x, behind, beyond)
            shifted = jnp.where(ahead_y, pltpu.roll(along, 1, 0), pltpu.roll(along, width_y - 1, 0))
            value = stay_y * along + b * shifted
            read[pl.ds(pl.multiple_of(x * width_y, 16), width_y), cut] = value.astype(read.dtype)

        def body(x, carry):
            behind, center = carry
            beyond = dev[x + 1, :, cut].astype(jnp.float32)
            one(x, behind, center, beyond)
            return center, beyond

        carry = (before[:, cut], dev[0, :, cut].astype(jnp.float32))
        behind, center = lax.fori_loop(0, width_x - 1, body, carry, unroll=4)
        one(width_x - 1, behind, center, after[:, cut])

    for fetch, store in moving:
        fetch.wait()
        store.start()
    head = read.shape[0] - extra.shape[0]
    tail_rows = read[head:, :]
    first = 0
    for out in outs:
        rows = slice(first, first + out.shape[0])
        first += out.shape[0]
        moved = jnp.dot(fill[rows, :], tail_rows, preferred_element_type=jnp.float32)
        kept = read[rows, :].astype(jnp.float32)
        out[...] = jnp.where(on_rim[rows, :] > 0, moved, kept).astype(out.dtype)
    extra[...] = jnp.dot(spare[...], tail_rows, preferred_element_type=jnp.float32).astype(extra.dtype)

    for store in stores:
        store.wait()


def payload_kernel(rows_of, cols_of, cells_lane, read, payload):
    slots, modes = payload.shape[2], read.shape[1]
    sub = jnp.broadcast_to(cells_lane[...], (128, slots)).T[:, 0:1]
    cell = lax.broadcasted_iota(jnp.int32, (slots, read.shape[0]), 1)
    select = (sub == cell).astype(jnp.float32).astype(jnp.bfloat16)
    rim = jnp.dot(select, read[...], preferred_element_type=jnp.float32)
    flipped = rim.T
    total = jnp.sum(flipped, axis=0, keepdims=True)
    high = total.astype(jnp.bfloat16).astype(jnp.float32)
    middle = (total - high).astype(jnp.bfloat16).astype(jnp.float32)
    low = total - high - middle
    place = lax.broadcasted_iota(jnp.int32, (TAIL, total.shape[1]), 0)
    tail = jnp.where(place == 0, high, jnp.where(place == 1, middle, jnp.where(place == 2, low, 0.0)))
    tail = tail.astype(jnp.bfloat16)
    piece = modes // (rows_of * cols_of)
    packed = flipped.astype(jnp.bfloat16)
    for r in range(rows_of):
        for c in range(cols_of):
            block = c * rows_of + r
            payload[r * cols_of + c, 0:piece, :] = packed[block * piece : (block + 1) * piece]
            payload[r * cols_of + c, piece : piece + TAIL, :] = tail


def rim_kernel(mode_count, specularity, arrived, mirror, wall, cells_lane, extra, out):
    groups, height, slots = arrived.shape
    piece = height - TAIL
    values = arrived[:, 0:piece, :].reshape(groups * piece, slots).T
    sums = arrived[:, piece:height, :].reshape(groups * TAIL, slots).astype(jnp.float32)
    total = jnp.broadcast_to(jnp.sum(sums, axis=0, keepdims=True), (128, slots)).T
    diffuse = total[:, 0:1] / mode_count
    walls = jnp.broadcast_to(wall[...], (128, slots)).T[:, 0:1]
    share = jnp.zeros(walls.shape, jnp.float32)
    mirrored = jnp.zeros(out.shape, jnp.float32)
    for w in range(mirror.shape[0]):
        share = jnp.where(walls == w, specularity[w], share)
        picked = jnp.dot(values, mirror[w], preferred_element_type=jnp.float32)
        mirrored = jnp.where(walls == w, picked, mirrored)
    emitted = share * mirrored + (1.0 - share) * diffuse
    used = jnp.broadcast_to(cells_lane[...], (128, slots)).T[:, 0:1] >= 0
    out[...] = jnp.where(used, emitted, extra[...].astype(jnp.float32)).astype(out.dtype)


def base_kernel(fill, on_rim, part, base):
    kept = part.shape[0]
    base[:kept, :] = jnp.where(on_rim[...] > 0, 0.0, part[...].astype(jnp.float32)).astype(base.dtype)
    moved = lax.dot_general(
        fill[...], part[...], (((0,), (0,)), ((), ())), preferred_element_type=jnp.float32
    )
    base[kept:, :] = moved.astype(base.dtype)


def merge_kernel(fill, spare, place, on_rim, base, total, from_left, from_right, out):
    slots = spare.shape[0]
    kept = base.shape[0] - slots
    total = total[...] + from_left[...].astype(jnp.float32) + from_right[...].astype(jnp.float32)
    total = total.astype(jnp.bfloat16)
    more = total.shape[0] - slots
    part, last = total[:more, :], total[more:, :]
    head = kept + more
    tn = (((0,), (0,)), ((), ()))
    moved = jnp.dot(place[:kept, :], last, preferred_element_type=jnp.float32)
    out[:kept, :] = (base[:kept, :].astype(jnp.float32) + moved).astype(out.dtype)
    moved = jnp.dot(place[kept:head, :], last, preferred_element_type=jnp.float32)
    out[kept:head, :] = jnp.where(on_rim[...] > 0, moved, part.astype(jnp.float32)).astype(out.dtype)
    moved = jnp.dot(place[head:, :], last, preferred_element_type=jnp.float32)
    moved = moved + lax.dot_general(spare[...], last, tn, preferred_element_type=jnp.float32)
    moved = moved + lax.dot_general(fill[...], part, tn, preferred_element_type=jnp.float32)
    out[head:, :] = (base[kept:, :].astype(jnp.float32) + moved).astype(out.dtype)


def hop_kernel(t, size, wide, slots, groups, has_recv, *refs):
    refs = list(refs)
    where = refs.pop(0)
    blocks = [[refs.pop(0) for _ in range(4)] for _ in range(groups)]
    own = refs.pop(0) if wide else None
    held = {j: (refs.pop(0), refs.pop(0)) for j in slots}
    final = t == size
    recv = [refs.pop(0), refs.pop(0)] if has_recv else None
    outs = [refs.pop(0)] if final else [refs.pop(0), refs.pop(0)]
    buffer, sem = refs
    s, r, c = where[0], where[1], where[2]
    rows = buffer.shape[1]
    width = blocks[0][0].shape[1]
    if final:
        jobs = [(c, None, size - 1)]
    else:
        first = slot_of(c, t, size)
        goes_right = c <= t - 1
        jobs = [
            (c + size - t, goes_right, first),
            (c - size + t, c >= size - t, first + jnp.where(goes_right, 1, 0)),
        ]

    def fetch(n, d, place):
        for b in range(4):
            source = lax.bitwise_xor(r, b)
            target = buffer.at[n, :, b * width : (b + 1) * width]
            if wide:
                column = pl.multiple_of(source * width, width)
                pltpu.make_async_copy(
                    own.at[pl.ds(pl.multiple_of(d * rows, rows), rows), pl.ds(column, width)],
                    target,
                    sem.at[n],
                ).start()
                continue
            column = pl.multiple_of(lax.bitwise_and(source, 1) * width, width)
            is_own = lax.shift_right_logical(source, 1) == s
            for j, pair in held.items():
                for use, shard in ((is_own, pair[0]), (jnp.logical_not(is_own), pair[1])):

                    @pl.when(jnp.logical_and(use, place == j))
                    def _(shard=shard):
                        pltpu.make_async_copy(shard.at[:, pl.ds(column, width)], target, sem.at[n]).start()

    def multiply(n, out):
        pltpu.make_async_copy(buffer.at[n], buffer.at[n], sem.at[n]).wait()
        first = 0
        for group in blocks:
            height = group[0].shape[0]
            for low in range(0, height, 384):
                inside = slice(low, min(low + 384, height))
                rows_here = slice(first + inside.start, first + inside.stop)
                total = None
                for b in range(4):
                    part = lax.dot_general(
                        group[b][inside, :],
                        buffer[n, :, b * width : (b + 1) * width],
                        NT,
                        preferred_element_type=jnp.float32,
                    )
                    total = part if total is None else total + part
                if final and has_recv:
                    total = total + recv[0][rows_here, :].astype(jnp.float32)
                    total = total + recv[1][rows_here, :].astype(jnp.float32)
                elif has_recv:
                    total = total + recv[n][rows_here, :].astype(jnp.float32)
                out[rows_here, :] = total.astype(out.dtype)
            first += height

    for n, (d, valid, place) in enumerate(jobs):
        if valid is None:
            fetch(n, d, place)
        else:
            pl.when(valid)(functools.partial(fetch, n, d, place))
    for n, (d, valid, place) in enumerate(jobs):
        if valid is None:
            multiply(n, outs[n])
        else:
            pl.when(valid)(functools.partial(multiply, n, outs[n]))


def hop(t, size, where, blocks, own, held, recv):
    wide = own is not None
    slots = () if wide else tuple(slots_at(t, size))
    rows = own.shape[0] // size if wide else held[0][0].shape[0]
    cells = sum(group[0].shape[0] for group in blocks)
    width = blocks[0][0].shape[1]
    count = 1 if t == size else 2
    kept = jnp.float32 if t == size and recv is None else jnp.bfloat16
    spec = pl.BlockSpec(memory_space=pltpu.VMEM)
    any_spec = pl.BlockSpec(memory_space=HBM)
    shards = [own] if wide else [shard for j in slots for shard in held[j]]
    operands = [where, *[block for group in blocks for block in group], *shards, *(recv or [])]
    in_specs = [pl.BlockSpec(memory_space=SMEM)] + [spec] * (4 * len(blocks)) + [any_spec] * len(shards)
    in_specs += [spec] * len(recv or [])
    return pl.pallas_call(
        functools.partial(hop_kernel, t, size, wide, slots, len(blocks), recv is not None),
        out_shape=[jax.ShapeDtypeStruct((cells, rows), kept)] * count,
        in_specs=in_specs,
        out_specs=[spec] * count,
        scratch_shapes=[
            pltpu.VMEM((count, rows, 4 * width), jnp.bfloat16),
            pltpu.SemaphoreType.DMA((count,)),
        ],
        compiler_params=pltpu.CompilerParams(vmem_limit_bytes=HOP_LIMIT),
        cost_estimate=takes(2 + cells / 300),
    )(*operands)


def on_device(deviation, courant, collide, hole_cells, hole_wall, specular, specularity):
    n_space, n_row, n_col = (lax.axis_size(name) for name in ("space", "mrow", "mcol"))
    s, r, c = (lax.axis_index(name) for name in ("space", "mrow", "mcol"))
    width_x, width_y, block_len = deviation.shape
    cell_count = width_x * width_y
    slot_count = hole_cells.shape[0]
    wall_count, mode_count = specular.shape
    piece = block_len // (n_row * n_col)
    groups = n_row * n_col
    vmem = pl.BlockSpec()
    hbm = pl.BlockSpec(memory_space=HBM)
    smem = pl.BlockSpec(memory_space=SMEM)
    params = pltpu.CompilerParams(vmem_limit_bytes=LIMIT)
    roomy = pltpu.CompilerParams(vmem_limit_bytes=24 * 1024 * 1024)
    where = jnp.stack([s, r, c]).astype(jnp.int32)

    if n_space == 2:
        edge = jnp.where(s == 0, deviation[-1:], deviation[:1])
        edges = [lax.ppermute(edge, "space", [(0, 1), (1, 0)])]
    else:
        up = [(i, i + 1) for i in range(n_space - 1)]
        down = [(j, i) for i, j in up]
        edges = [lax.ppermute(deviation[-1:], "space", up), lax.ppermute(deviation[:1], "space", down)]

    def after(value, *first):
        return lax.optimization_barrier((value, first))[0]

    def shape(*dims):
        return jax.ShapeDtypeStruct(dims, jnp.bfloat16)

    head = cell_count - slot_count
    sizes = [head * part // sum(SPLIT) for part in SPLIT]
    count = len(sizes)
    lane_cells = hole_cells[None, :]
    wide = n_space != 2
    rows = collide.shape[0] // n_col
    own = lax.all_gather(collide, "space", axis=1, tiled=True) if wide else None
    shards = 0 if wide else n_col
    swap = [(0, 1), (1, 0)]
    held, order = [], jnp.asarray(line_steps(n_col))
    extra, *mine = pl.pallas_call(
        functools.partial(read_kernel, count, shards),
        out_shape=[shape(slot_count, block_len)]
        + [shape(size, block_len) for size in sizes]
        + [shape(rows, collide.shape[1])] * shards
        + [shape(cell_count, block_len)],
        in_specs=[smem] + [vmem] * (3 + len(edges)) + [smem, hbm][: shards * 2],
        out_specs=[vmem] * (count + 1) + [hbm] * shards + [vmem],
        scratch_shapes=[
            pltpu.VMEM((head, slot_count), jnp.bfloat16),
            pltpu.VMEM((slot_count, slot_count), jnp.bfloat16),
            pltpu.VMEM((head, 1), jnp.float32),
        ]
        + [
            pltpu.VMEM((shards, rows, collide.shape[1]), jnp.bfloat16),
            pltpu.SemaphoreType.DMA((shards,)),
            pltpu.SemaphoreType.DMA((shards,)),
        ][: shards * 3],
        compiler_params=params,
        cost_estimate=takes(6),
    )(where, deviation, courant, lane_cells, *edges, *([] if wide else [order, collide]))
    read = mine.pop()
    payload = pl.pallas_call(
        functools.partial(payload_kernel, n_row, n_col),
        out_shape=shape(groups, piece + TAIL, slot_count),
        in_specs=[vmem] * 2,
        out_specs=vmem,
        compiler_params=params,
        cost_estimate=takes(3),
    )(lane_cells, read)
    mine, parts = mine[:count], mine[count:]
    for part in parts:
        held.append((part, lax.ppermute(part, "space", swap)))

    flip = [[(i, i ^ bit) for i in range(n_row)] for bit in (1, 2)]
    right = [(i, i + 1) for i in range(n_col - 1)]
    left = [(j, i) for i, j in right]
    far = []
    for value in mine:
        far.append(lax.ppermute(value, "mrow", flip[1]))
    arrived = lax.all_to_all(payload, ("mrow", "mcol"), split_axis=0, concat_axis=0, tiled=True)
    def send(t, value):
        return [
            lax.ppermute(value[0], "mcol", right[:t]),
            lax.ppermute(value[1], "mcol", left[n_col - 1 - t :]),
        ]

    state = {}
    done = ()

    def step(t, n, *ready):
        return hop(t, n_col, after(where, *done, *ready), chunks[n], own, held, state.get(n))

    def gather(n):
        near = lax.ppermute(mine[n], "mrow", flip[0])
        both = lax.ppermute(after(far[n], *done), "mrow", flip[0])
        return [mine[n], near, far[n], both]

    own_table = lax.dynamic_slice_in_dim(specular, (c * n_row + r) * block_len, block_len, 1)
    mirror, place, spare, fill, fill_more, on_rim, on_rim_more = pl.pallas_call(
        functools.partial(late_mask_kernel, n_row, n_col),
        out_shape=[
            shape(wall_count, block_len, block_len),
            shape(cell_count, slot_count),
            shape(slot_count, slot_count),
            *[shape(size, slot_count) for size in sizes],
            *[jax.ShapeDtypeStruct((size, 1), jnp.float32) for size in sizes],
        ],
        in_specs=[vmem] * 2,
        out_specs=[vmem] * 7,
        scratch_shapes=[pltpu.VMEM((head, slot_count), jnp.bfloat16), pltpu.VMEM((head, 1), jnp.float32)],
        compiler_params=params,
        cost_estimate=takes(4),
    )(after(lane_cells, extra), own_table)
    far[0] = after(far[0], mirror, *[other for _, other in held[:1]])
    chunks = [[gather(0)]]
    done = step(1, 0, arrived)
    state[0] = send(1, done)
    mine.append(
        pl.pallas_call(
            functools.partial(rim_kernel, mode_count),
            out_shape=shape(slot_count, block_len),
            in_specs=[smem] + [vmem] * 5,
            out_specs=vmem,
            compiler_params=roomy,
            cost_estimate=takes(4),
        )(specularity, after(arrived, far[1], *done), mirror, hole_wall[None, :], lane_cells, extra)
    )
    far.append(lax.ppermute(mine[count], "mrow", flip[1]))
    chunks.append([gather(n) for n in range(1, count + 1)])
    done = step(1, 1, *state[0])
    state[1] = send(1, done)
    outs = []
    for t in range(2, n_col + 1):
        for n in (0, 1):
            if (t, n) == (n_col, 1):
                continue
            done = step(t, n)
            if t == n_col:
                outs.append(done[0])
            else:
                state[n] = send(t, done)
    total = hop(n_col, n_col, after(where, *done), chunks[1], own, held, None)[0]
    base = pl.pallas_call(
        base_kernel,
        out_shape=shape(sizes[0] + slot_count, rows),
        in_specs=[vmem] * 3,
        out_specs=vmem,
        compiler_params=roomy,
        cost_estimate=takes(2),
    )(fill, on_rim, *outs)
    near = pl.BlockSpec(memory_space=pltpu.VMEM)
    out = pl.pallas_call(
        merge_kernel,
        out_shape=shape(cell_count, rows),
        in_specs=[near] * 8,
        out_specs=vmem,
        compiler_params=pltpu.CompilerParams(vmem_limit_bytes=HOP_LIMIT),
        cost_estimate=takes(4),
    )(fill_more, spare, place, on_rim_more, base, total, *state[1])
    return out.reshape(width_x, width_y, rows)


def solution(mesh):
    in_specs = (
        P("space", None, ("mcol", "mrow")),
        P(None, ("mcol", "mrow")),
        P("mrow", ("mcol", "space")),
        P("space"),
        P("space"),
        P(),
        P(),
    )
    out_specs = P("space", None, ("mrow", "mcol"))
    return jax.shard_map(
        on_device, mesh=mesh, in_specs=in_specs, out_specs=out_specs, check_vma=False
    )
```

```python
import functools
import jax
import jax.numpy as jnp
import numpy as np
from jax import lax
from jax.experimental import pallas as pl
from jax.experimental.pallas import tpu as pltpu
from jax.sharding import PartitionSpec as P

SMEM = pltpu.SMEM
HBM = pltpu.HBM
NT = (((1,), (1,)), ((), ()))
SPLIT = (2, 1)
LIMIT = 60 * 1024 * 1024
HOP_LIMIT = 16 * 1024 * 1024


def takes(microseconds):
    return pl.CostEstimate(flops=int(microseconds * 0.5e9), bytes_accessed=0, transcendentals=0)


TAIL = 16


def line_steps(size):
    order = []
    for c in range(size):
        row = []
        for t in range(1, size):
            if c <= t - 1:
                row.append(c + size - t)
            if c >= size - t:
                row.append(c - size + t)
        row.append(c)
        order.append(row)
    return np.array(order, np.int32)


def slot_of(c, t, size):
    place = 0
    for u in range(1, t):
        place = place + jnp.where(c <= u - 1, 1, 0) + jnp.where(c >= size - u, 1, 0)
    return place


def slots_at(t, size):
    found = set()
    for c in range(size):
        place = 0
        for u in range(1, size):
            for hit in (c <= u - 1, c >= size - u):
                if hit:
                    if u == t:
                        found.add(place)
                    place += 1
        if t == size:
            found.add(size - 1)
    return sorted(found)


def moves(lane, head, fill, spare, on_rim):
    slots = lane.shape[1]
    sub = jnp.broadcast_to(lane, (128, slots)).T[:, 0:1]
    total = jnp.sum((lane >= 0).astype(jnp.float32), axis=1, keepdims=True).astype(jnp.int32)
    in_head = jnp.logical_and(lane >= 0, lane < head)
    head_count = jnp.sum(in_head.astype(jnp.float32), axis=1, keepdims=True).astype(jnp.int32)
    place = lax.broadcasted_iota(jnp.int32, (1, slots), 1)
    tail = jnp.broadcast_to(place + head, (slots, slots))
    wide_sub = jnp.broadcast_to(sub, (slots, slots))
    before = jnp.logical_and(wide_sub >= head, wide_sub < tail).astype(jnp.float32)
    hit = (wide_sub == tail).astype(jnp.float32)
    rank = place - jnp.sum(before, axis=0, keepdims=True).astype(jnp.int32)
    tail_key = jnp.where(jnp.sum(hit, axis=0, keepdims=True) > 0, -2, rank)
    row = lax.broadcasted_iota(jnp.int32, (head, slots), 0)
    wide_lane = jnp.broadcast_to(lane, (head, slots))
    ahead = jnp.logical_and(wide_lane >= 0, wide_lane < row).astype(jnp.float32)
    hits = jnp.max((wide_lane == row).astype(jnp.float32), axis=1, keepdims=True)
    head_key = jnp.where(hits > 0, jnp.sum(ahead, axis=1, keepdims=True).astype(jnp.int32), -1)
    on_rim[...] = hits
    fill[...] = (head_key == tail_key).astype(jnp.float32).astype(jnp.bfloat16)
    slot = lax.broadcasted_iota(jnp.int32, (slots, 1), 0)
    slot_key = jnp.where(slot >= total, slot - total + head_count, -1)
    spare[...] = (slot_key == tail_key).astype(jnp.float32).astype(jnp.bfloat16)
    return sub


def late_mask_kernel(
    rows_of, cols_of, cells_lane, table, mirror, place, spare, fill, fill_more, on_rim, on_rim_more, fills, flags
):
    cell = lax.broadcasted_iota(jnp.int32, place.shape, 0)
    place[...] = (cells_lane[...] == cell).astype(jnp.float32).astype(jnp.bfloat16)
    modes = mirror.shape[1]
    piece = modes // (rows_of * cols_of)
    entry = table[...]
    block = lax.div(entry, modes)
    group = lax.rem(block, rows_of) * cols_of + lax.div(block, rows_of)
    position = group * piece + lax.rem(entry, piece)
    source = lax.broadcasted_iota(jnp.int32, mirror.shape[1:], 0)
    for w in range(mirror.shape[0]):
        mirror[w] = (position[w : w + 1] == source).astype(jnp.float32).astype(jnp.bfloat16)
    moves(cells_lane[...], fills.shape[0], fills, spare, flags)
    kept = fill.shape[0]
    fill[...] = fills[:kept, :]
    fill_more[...] = fills[kept:, :]
    on_rim[...] = flags[:kept, :]
    on_rim_more[...] = flags[kept:, :]


def read_kernel(count, shards, *refs):
    refs = list(refs)
    where, dev, courant, cells_lane = (refs.pop(0) for _ in range(4))
    edges = [refs.pop(0) for _ in range(2 if not shards else 1)]
    table, whole = (refs.pop(0) for _ in range(2)) if shards else (None, None)
    extra = refs.pop(0)
    outs = [refs.pop(0) for _ in range(count)]
    parts = [refs.pop(0) for _ in range(shards)]
    read, fill, spare, on_rim = (refs.pop(0) for _ in range(4))
    fetches, stores = [], []
    if shards:
        stage, in_sem, out_sem = refs
        rows = stage.shape[1]
        for j in range(shards):
            first = pl.multiple_of(table[where[2], j] * rows, rows)
            fetches.append(
                pltpu.make_async_copy(whole.at[pl.ds(first, rows), :], stage.at[j], in_sem.at[j])
            )
            stores.append(pltpu.make_async_copy(stage.at[j], parts[j], out_sem.at[j]))
    for copy in fetches:
        copy.start()
    moves(cells_lane[...], fill.shape[0], fill, spare, on_rim)
    width_x, width_y, modes = dev.shape
    speed = courant[...]
    reach = jnp.abs(speed)
    ahead = jnp.where(speed > 0, 1.0, 0.0)
    if shards:
        edge = edges[0][0].astype(jnp.float32)
        before, after = jnp.where(where[0] == 1, edge, 0.0), jnp.where(where[0] == 0, edge, 0.0)
    else:
        before, after = edges[0][0].astype(jnp.float32), edges[1][0].astype(jnp.float32)
    lanes = 128
    moving = list(zip(fetches, stores))
    for low in range(0, modes, lanes):
        if low and moving:
            fetch, store = moving.pop(0)
            fetch.wait()
            store.start()
        cut = slice(low, low + lanes)
        a, b = reach[0:1, cut], reach[1:2, cut]
        stay_x, stay_y = 1.0 - a, 1.0 - b
        ahead_x = jnp.broadcast_to(ahead[0:1, cut], (width_y, lanes)) > 0
        ahead_y = jnp.broadcast_to(ahead[1:2, cut], (width_y, lanes)) > 0

        def one(x, behind, center, beyond):
            along = stay_x * center + a * jnp.where(ahead_x, behind, beyond)
            shifted = jnp.where(ahead_y, pltpu.roll(along, 1, 0), pltpu.roll(along, width_y - 1, 0))
            value = stay_y * along + b * shifted
            read[pl.ds(pl.multiple_of(x * width_y, 16), width_y), cut] = value.astype(read.dtype)

        def body(x, carry):
            behind, center = carry
            beyond = dev[x + 1, :, cut].astype(jnp.float32)
            one(x, behind, center, beyond)
            return center, beyond

        carry = (before[:, cut], dev[0, :, cut].astype(jnp.float32))
        behind, center = lax.fori_loop(0, width_x - 1, body, carry, unroll=4)
        one(width_x - 1, behind, center, after[:, cut])

    for fetch, store in moving:
        fetch.wait()
        store.start()
    head = read.shape[0] - extra.shape[0]
    tail_rows = read[head:, :]
    first = 0
    for out in outs:
        rows = slice(first, first + out.shape[0])
        first += out.shape[0]
        moved = jnp.dot(fill[rows, :], tail_rows, preferred_element_type=jnp.float32)
        kept = read[rows, :].astype(jnp.float32)
        out[...] = jnp.where(on_rim[rows, :] > 0, moved, kept).astype(out.dtype)
    extra[...] = jnp.dot(spare[...], tail_rows, preferred_element_type=jnp.float32).astype(extra.dtype)

    for store in stores:
        store.wait()


def payload_kernel(rows_of, cols_of, cells_lane, read, payload):
    slots, modes = payload.shape[2], read.shape[1]
    sub = jnp.broadcast_to(cells_lane[...], (128, slots)).T[:, 0:1]
    cell = lax.broadcasted_iota(jnp.int32, (slots, read.shape[0]), 1)
    select = (sub == cell).astype(jnp.float32).astype(jnp.bfloat16)
    rim = jnp.dot(select, read[...], preferred_element_type=jnp.float32)
    flipped = rim.T
    total = jnp.sum(flipped, axis=0, keepdims=True)
    high = total.astype(jnp.bfloat16).astype(jnp.float32)
    middle = (total - high).astype(jnp.bfloat16).astype(jnp.float32)
    low = total - high - middle
    place = lax.broadcasted_iota(jnp.int32, (TAIL, total.shape[1]), 0)
    tail = jnp.where(place == 0, high, jnp.where(place == 1, middle, jnp.where(place == 2, low, 0.0)))
    tail = tail.astype(jnp.bfloat16)
    piece = modes // (rows_of * cols_of)
    packed = flipped.astype(jnp.bfloat16)
    for r in range(rows_of):
        for c in range(cols_of):
            block = c * rows_of + r
            payload[r * cols_of + c, 0:piece, :] = packed[block * piece : (block + 1) * piece]
            payload[r * cols_of + c, piece : piece + TAIL, :] = tail


def rim_kernel(mode_count, specularity, arrived, mirror, wall, cells_lane, extra, out):
    groups, height, slots = arrived.shape
    piece = height - TAIL
    values = arrived[:, 0:piece, :].reshape(groups * piece, slots).T
    sums = arrived[:, piece:height, :].reshape(groups * TAIL, slots).astype(jnp.float32)
    total = jnp.broadcast_to(jnp.sum(sums, axis=0, keepdims=True), (128, slots)).T
    diffuse = total[:, 0:1] / mode_count
    walls = jnp.broadcast_to(wall[...], (128, slots)).T[:, 0:1]
    share = jnp.zeros(walls.shape, jnp.float32)
    mirrored = jnp.zeros(out.shape, jnp.float32)
    for w in range(mirror.shape[0]):
        share = jnp.where(walls == w, specularity[w], share)
        picked = jnp.dot(values, mirror[w], preferred_element_type=jnp.float32)
        mirrored = jnp.where(walls == w, picked, mirrored)
    emitted = share * mirrored + (1.0 - share) * diffuse
    used = jnp.broadcast_to(cells_lane[...], (128, slots)).T[:, 0:1] >= 0
    out[...] = jnp.where(used, emitted, extra[...].astype(jnp.float32)).astype(out.dtype)


def base_kernel(fill, on_rim, part, base):
    kept = part.shape[0]
    base[:kept, :] = jnp.where(on_rim[...] > 0, 0.0, part[...].astype(jnp.float32)).astype(base.dtype)
    moved = lax.dot_general(
        fill[...], part[...], (((0,), (0,)), ((), ())), preferred_element_type=jnp.float32
    )
    base[kept:, :] = moved.astype(base.dtype)


def merge_kernel(fill, spare, place, on_rim, base, total, from_left, from_right, out):
    slots = spare.shape[0]
    kept = base.shape[0] - slots
    total = total[...] + from_left[...].astype(jnp.float32) + from_right[...].astype(jnp.float32)
    total = total.astype(jnp.bfloat16)
    more = total.shape[0] - slots
    part, last = total[:more, :], total[more:, :]
    head = kept + more
    tn = (((0,), (0,)), ((), ()))
    moved = jnp.dot(place[:kept, :], last, preferred_element_type=jnp.float32)
    out[:kept, :] = (base[:kept, :].astype(jnp.float32) + moved).astype(out.dtype)
    moved = jnp.dot(place[kept:head, :], last, preferred_element_type=jnp.float32)
    out[kept:head, :] = jnp.where(on_rim[...] > 0, moved, part.astype(jnp.float32)).astype(out.dtype)
    moved = jnp.dot(place[head:, :], last, preferred_element_type=jnp.float32)
    moved = moved + lax.dot_general(spare[...], last, tn, preferred_element_type=jnp.float32)
    moved = moved + lax.dot_general(fill[...], part, tn, preferred_element_type=jnp.float32)
    out[head:, :] = (base[kept:, :].astype(jnp.float32) + moved).astype(out.dtype)


def hop_kernel(t, size, wide, slots, groups, has_recv, *refs):
    refs = list(refs)
    where = refs.pop(0)
    blocks = [[refs.pop(0) for _ in range(4)] for _ in range(groups)]
    own = refs.pop(0) if wide else None
    held = {j: (refs.pop(0), refs.pop(0)) for j in slots}
    final = t == size
    recv = [refs.pop(0), refs.pop(0)] if has_recv else None
    outs = [refs.pop(0)] if final else [refs.pop(0), refs.pop(0)]
    buffer, sem = refs
    s, r, c = where[0], where[1], where[2]
    rows = buffer.shape[1]
    width = blocks[0][0].shape[1]
    if final:
        jobs = [(c, None, size - 1)]
    else:
        first = slot_of(c, t, size)
        goes_right = c <= t - 1
        jobs = [
            (c + size - t, goes_right, first),
            (c - size + t, c >= size - t, first + jnp.where(goes_right, 1, 0)),
        ]

    def fetch(n, d, place):
        for b in range(4):
            source = lax.bitwise_xor(r, b)
            target = buffer.at[n, :, b * width : (b + 1) * width]
            if wide:
                column = pl.multiple_of(source * width, width)
                pltpu.make_async_copy(
                    own.at[pl.ds(pl.multiple_of(d * rows, rows), rows), pl.ds(column, width)],
                    target,
                    sem.at[n],
                ).start()
                continue
            column = pl.multiple_of(lax.bitwise_and(source, 1) * width, width)
            is_own = lax.shift_right_logical(source, 1) == s
            for j, pair in held.items():
                for use, shard in ((is_own, pair[0]), (jnp.logical_not(is_own), pair[1])):

                    @pl.when(jnp.logical_and(use, place == j))
                    def _(shard=shard):
                        pltpu.make_async_copy(shard.at[:, pl.ds(column, width)], target, sem.at[n]).start()

    def multiply(n, out):
        pltpu.make_async_copy(buffer.at[n], buffer.at[n], sem.at[n]).wait()
        first = 0
        for group in blocks:
            height = group[0].shape[0]
            tile = min(384, height)

            def rows_of_tile(i, carry, group=group, first=first, tile=tile):
                low = pl.multiple_of(i * tile, tile)
                inside, rows_here = pl.ds(low, tile), pl.ds(first + low, tile)
                total = None
                for b in range(4):
                    part = lax.dot_general(
                        group[b][inside, :],
                        buffer[n, :, b * width : (b + 1) * width],
                        NT,
                        preferred_element_type=jnp.float32,
                    )
                    total = part if total is None else total + part
                if final and has_recv:
                    total = total + recv[0][rows_here, :].astype(jnp.float32)
                    total = total + recv[1][rows_here, :].astype(jnp.float32)
                elif has_recv:
                    total = total + recv[n][rows_here, :].astype(jnp.float32)
                out[rows_here, :] = total.astype(out.dtype)
                return carry

            lax.fori_loop(0, height // tile, rows_of_tile, 0)
            first += height

    for n, (d, valid, place) in enumerate(jobs):
        if valid is None:
            fetch(n, d, place)
        else:
            pl.when(valid)(functools.partial(fetch, n, d, place))
    for n, (d, valid, place) in enumerate(jobs):
        if valid is None:
            multiply(n, outs[n])
        else:
            pl.when(valid)(functools.partial(multiply, n, outs[n]))


def hop(t, size, where, blocks, own, held, recv):
    wide = own is not None
    slots = () if wide else tuple(slots_at(t, size))
    rows = own.shape[0] // size if wide else held[0][0].shape[0]
    cells = sum(group[0].shape[0] for group in blocks)
    width = blocks[0][0].shape[1]
    count = 1 if t == size else 2
    kept = jnp.float32 if t == size and recv is None else jnp.bfloat16
    spec = pl.BlockSpec(memory_space=pltpu.VMEM)
    any_spec = pl.BlockSpec(memory_space=HBM)
    shards = [own] if wide else [shard for j in slots for shard in held[j]]
    operands = [where, *[block for group in blocks for block in group], *shards, *(recv or [])]
    in_specs = [pl.BlockSpec(memory_space=SMEM)] + [spec] * (4 * len(blocks)) + [any_spec] * len(shards)
    in_specs += [spec] * len(recv or [])
    return pl.pallas_call(
        functools.partial(hop_kernel, t, size, wide, slots, len(blocks), recv is not None),
        out_shape=[jax.ShapeDtypeStruct((cells, rows), kept)] * count,
        in_specs=in_specs,
        out_specs=[spec] * count,
        scratch_shapes=[
            pltpu.VMEM((count, rows, 4 * width), jnp.bfloat16),
            pltpu.SemaphoreType.DMA((count,)),
        ],
        compiler_params=pltpu.CompilerParams(vmem_limit_bytes=HOP_LIMIT),
        cost_estimate=takes(2 + cells / 300),
    )(*operands)


def on_device(deviation, courant, collide, hole_cells, hole_wall, specular, specularity):
    n_space, n_row, n_col = (lax.axis_size(name) for name in ("space", "mrow", "mcol"))
    s, r, c = (lax.axis_index(name) for name in ("space", "mrow", "mcol"))
    width_x, width_y, block_len = deviation.shape
    cell_count = width_x * width_y
    slot_count = hole_cells.shape[0]
    wall_count, mode_count = specular.shape
    piece = block_len // (n_row * n_col)
    groups = n_row * n_col
    vmem = pl.BlockSpec()
    hbm = pl.BlockSpec(memory_space=HBM)
    smem = pl.BlockSpec(memory_space=SMEM)
    params = pltpu.CompilerParams(vmem_limit_bytes=LIMIT)
    roomy = pltpu.CompilerParams(vmem_limit_bytes=24 * 1024 * 1024)
    where = jnp.stack([s, r, c]).astype(jnp.int32)

    if n_space == 2:
        edge = jnp.where(s == 0, deviation[-1:], deviation[:1])
        edges = [lax.ppermute(edge, "space", [(0, 1), (1, 0)])]
    else:
        up = [(i, i + 1) for i in range(n_space - 1)]
        down = [(j, i) for i, j in up]
        edges = [lax.ppermute(deviation[-1:], "space", up), lax.ppermute(deviation[:1], "space", down)]

    def after(value, *first):
        return lax.optimization_barrier((value, first))[0]

    def shape(*dims):
        return jax.ShapeDtypeStruct(dims, jnp.bfloat16)

    head = cell_count - slot_count
    sizes = [head * part // sum(SPLIT) for part in SPLIT]
    count = len(sizes)
    lane_cells = hole_cells[None, :]
    wide = n_space != 2
    rows = collide.shape[0] // n_col
    own = lax.all_gather(collide, "space", axis=1, tiled=True) if wide else None
    shards = 0 if wide else n_col
    swap = [(0, 1), (1, 0)]
    held, order = [], jnp.asarray(line_steps(n_col))
    extra, *mine = pl.pallas_call(
        functools.partial(read_kernel, count, shards),
        out_shape=[shape(slot_count, block_len)]
        + [shape(size, block_len) for size in sizes]
        + [shape(rows, collide.shape[1])] * shards
        + [shape(cell_count, block_len)],
        in_specs=[smem] + [vmem] * (3 + len(edges)) + [smem, hbm][: shards * 2],
        out_specs=[vmem] * (count + 1) + [hbm] * shards + [vmem],
        scratch_shapes=[
            pltpu.VMEM((head, slot_count), jnp.bfloat16),
            pltpu.VMEM((slot_count, slot_count), jnp.bfloat16),
            pltpu.VMEM((head, 1), jnp.float32),
        ]
        + [
            pltpu.VMEM((shards, rows, collide.shape[1]), jnp.bfloat16),
            pltpu.SemaphoreType.DMA((shards,)),
            pltpu.SemaphoreType.DMA((shards,)),
        ][: shards * 3],
        compiler_params=params,
        cost_estimate=takes(6),
    )(where, deviation, courant, lane_cells, *edges, *([] if wide else [order, collide]))
    read = mine.pop()
    payload = pl.pallas_call(
        functools.partial(payload_kernel, n_row, n_col),
        out_shape=shape(groups, piece + TAIL, slot_count),
        in_specs=[vmem] * 2,
        out_specs=vmem,
        compiler_params=params,
        cost_estimate=takes(3),
    )(lane_cells, read)
    mine, parts = mine[:count], mine[count:]
    for part in parts:
        held.append((part, lax.ppermute(part, "space", swap)))

    flip = [[(i, i ^ bit) for i in range(n_row)] for bit in (1, 2)]
    right = [(i, i + 1) for i in range(n_col - 1)]
    left = [(j, i) for i, j in right]
    far = []
    for value in mine:
        far.append(lax.ppermute(value, "mrow", flip[1]))
    arrived = lax.all_to_all(payload, ("mrow", "mcol"), split_axis=0, concat_axis=0, tiled=True)
    def send(t, value):
        return [
            lax.ppermute(value[0], "mcol", right[:t]),
            lax.ppermute(value[1], "mcol", left[n_col - 1 - t :]),
        ]

    state = {}
    done = ()

    def step(t, n, *ready):
        return hop(t, n_col, after(where, *done, *ready), chunks[n], own, held, state.get(n))

    def gather(n):
        near = lax.ppermute(mine[n], "mrow", flip[0])
        both = lax.ppermute(after(far[n], *done), "mrow", flip[0])
        return [mine[n], near, far[n], both]

    own_table = lax.dynamic_slice_in_dim(specular, (c * n_row + r) * block_len, block_len, 1)
    mirror, place, spare, fill, fill_more, on_rim, on_rim_more = pl.pallas_call(
        functools.partial(late_mask_kernel, n_row, n_col),
        out_shape=[
            shape(wall_count, block_len, block_len),
            shape(cell_count, slot_count),
            shape(slot_count, slot_count),
            *[shape(size, slot_count) for size in sizes],
            *[jax.ShapeDtypeStruct((size, 1), jnp.float32) for size in sizes],
        ],
        in_specs=[vmem] * 2,
        out_specs=[vmem] * 7,
        scratch_shapes=[pltpu.VMEM((head, slot_count), jnp.bfloat16), pltpu.VMEM((head, 1), jnp.float32)],
        compiler_params=params,
        cost_estimate=takes(4),
    )(after(lane_cells, extra), own_table)
    far[0] = after(far[0], mirror, *[other for _, other in held[:1]])
    chunks = [[gather(0)]]
    done = step(1, 0, arrived)
    state[0] = send(1, done)
    mine.append(
        pl.pallas_call(
            functools.partial(rim_kernel, mode_count),
            out_shape=shape(slot_count, block_len),
            in_specs=[smem] + [vmem] * 5,
            out_specs=vmem,
            compiler_params=roomy,
            cost_estimate=takes(4),
        )(specularity, after(arrived, far[1], *done), mirror, hole_wall[None, :], lane_cells, extra)
    )
    far.append(lax.ppermute(mine[count], "mrow", flip[1]))
    chunks.append([gather(n) for n in range(1, count + 1)])
    done = step(1, 1, *state[0])
    state[1] = send(1, done)
    outs = []
    for t in range(2, n_col + 1):
        for n in (0, 1):
            if (t, n) == (n_col, 1):
                continue
            done = step(t, n)
            if t == n_col:
                outs.append(done[0])
            else:
                state[n] = send(t, done)
    total = hop(n_col, n_col, after(where, *done), chunks[1], own, held, None)[0]
    base = pl.pallas_call(
        base_kernel,
        out_shape=shape(sizes[0] + slot_count, rows),
        in_specs=[vmem] * 3,
        out_specs=vmem,
        compiler_params=roomy,
        cost_estimate=takes(2),
    )(fill, on_rim, *outs)
    near = pl.BlockSpec(memory_space=pltpu.VMEM)
    out = pl.pallas_call(
        merge_kernel,
        out_shape=shape(cell_count, rows),
        in_specs=[near] * 8,
        out_specs=vmem,
        compiler_params=pltpu.CompilerParams(vmem_limit_bytes=HOP_LIMIT),
        cost_estimate=takes(4),
    )(fill_more, spare, place, on_rim_more, base, total, *state[1])
    return out.reshape(width_x, width_y, rows)


def solution(mesh):
    in_specs = (
        P("space", None, ("mcol", "mrow")),
        P(None, ("mcol", "mrow")),
        P("mrow", ("mcol", "space")),
        P("space"),
        P("space"),
        P(),
        P(),
    )
    out_specs = P("space", None, ("mrow", "mcol"))
    return jax.shard_map(
        on_device, mesh=mesh, in_specs=in_specs, out_specs=out_specs, check_vma=False
    )
```

```python
import functools
import jax
import jax.numpy as jnp
import numpy as np
from jax import lax
from jax.experimental import pallas as pl
from jax.experimental.pallas import tpu as pltpu
from jax.sharding import PartitionSpec as P

SMEM = pltpu.SMEM
HBM = pltpu.HBM
NT = (((1,), (1,)), ((), ()))
SPLIT = (2, 1)
LIMIT = 60 * 1024 * 1024
HOP_LIMIT = 16 * 1024 * 1024


def takes(microseconds):
    return pl.CostEstimate(flops=int(microseconds * 0.5e9), bytes_accessed=0, transcendentals=0)


TAIL = 16


def line_steps(size):
    order = []
    for c in range(size):
        row = []
        for t in range(1, size):
            if c <= t - 1:
                row.append(c + size - t)
            if c >= size - t:
                row.append(c - size + t)
        row.append(c)
        order.append(row)
    return np.array(order, np.int32)


def slot_of(c, t, size):
    place = 0
    for u in range(1, t):
        place = place + jnp.where(c <= u - 1, 1, 0) + jnp.where(c >= size - u, 1, 0)
    return place


def slots_at(t, size):
    found = set()
    for c in range(size):
        place = 0
        for u in range(1, size):
            for hit in (c <= u - 1, c >= size - u):
                if hit:
                    if u == t:
                        found.add(place)
                    place += 1
        if t == size:
            found.add(size - 1)
    return sorted(found)


def moves(lane, head, fill, spare, on_rim):
    slots = lane.shape[1]
    sub = jnp.broadcast_to(lane, (128, slots)).T[:, 0:1]
    total = jnp.sum((lane >= 0).astype(jnp.float32), axis=1, keepdims=True).astype(jnp.int32)
    in_head = jnp.logical_and(lane >= 0, lane < head)
    head_count = jnp.sum(in_head.astype(jnp.float32), axis=1, keepdims=True).astype(jnp.int32)
    place = lax.broadcasted_iota(jnp.int32, (1, slots), 1)
    tail = jnp.broadcast_to(place + head, (slots, slots))
    wide_sub = jnp.broadcast_to(sub, (slots, slots))
    before = jnp.logical_and(wide_sub >= head, wide_sub < tail).astype(jnp.float32)
    hit = (wide_sub == tail).astype(jnp.float32)
    rank = place - jnp.sum(before, axis=0, keepdims=True).astype(jnp.int32)
    tail_key = jnp.where(jnp.sum(hit, axis=0, keepdims=True) > 0, -2, rank)
    row = lax.broadcasted_iota(jnp.int32, (head, slots), 0)
    wide_lane = jnp.broadcast_to(lane, (head, slots))
    ahead = jnp.logical_and(wide_lane >= 0, wide_lane < row).astype(jnp.float32)
    hits = jnp.max((wide_lane == row).astype(jnp.float32), axis=1, keepdims=True)
    head_key = jnp.where(hits > 0, jnp.sum(ahead, axis=1, keepdims=True).astype(jnp.int32), -1)
    on_rim[...] = hits
    fill[...] = (head_key == tail_key).astype(jnp.float32).astype(jnp.bfloat16)
    slot = lax.broadcasted_iota(jnp.int32, (slots, 1), 0)
    slot_key = jnp.where(slot >= total, slot - total + head_count, -1)
    spare[...] = (slot_key == tail_key).astype(jnp.float32).astype(jnp.bfloat16)
    return sub


def late_mask_kernel(
    rows_of, cols_of, cells_lane, table, mirror, place, spare, fill, fill_more, on_rim, on_rim_more, fills, flags
):
    cell = lax.broadcasted_iota(jnp.int32, place.shape, 0)
    place[...] = (cells_lane[...] == cell).astype(jnp.float32).astype(jnp.bfloat16)
    modes = mirror.shape[1]
    piece = modes // (rows_of * cols_of)
    entry = table[...]
    block = lax.div(entry, modes)
    group = lax.rem(block, rows_of) * cols_of + lax.div(block, rows_of)
    position = group * piece + lax.rem(entry, piece)
    source = lax.broadcasted_iota(jnp.int32, mirror.shape[1:], 0)
    for w in range(mirror.shape[0]):
        mirror[w] = (position[w : w + 1] == source).astype(jnp.float32).astype(jnp.bfloat16)
    moves(cells_lane[...], fills.shape[0], fills, spare, flags)
    kept = fill.shape[0]
    fill[...] = fills[:kept, :]
    fill_more[...] = fills[kept:, :]
    on_rim[...] = flags[:kept, :]
    on_rim_more[...] = flags[kept:, :]


def read_kernel(count, shards, *refs):
    refs = list(refs)
    where, dev, courant, cells_lane = (refs.pop(0) for _ in range(4))
    edges = [refs.pop(0) for _ in range(2 if not shards else 1)]
    table, whole = (refs.pop(0) for _ in range(2)) if shards else (None, None)
    extra = refs.pop(0)
    outs = [refs.pop(0) for _ in range(count)]
    parts = [refs.pop(0) for _ in range(shards)]
    read, fill, spare, on_rim = (refs.pop(0) for _ in range(4))
    fetches, stores = [], []
    if shards:
        stage, in_sem, out_sem = refs
        rows = stage.shape[1]
        for j in range(shards):
            first = pl.multiple_of(table[where[2], j] * rows, rows)
            fetches.append(
                pltpu.make_async_copy(whole.at[pl.ds(first, rows), :], stage.at[j], in_sem.at[j])
            )
            stores.append(pltpu.make_async_copy(stage.at[j], parts[j], out_sem.at[j]))
    for copy in fetches:
        copy.start()
    moves(cells_lane[...].reshape(1, -1), fill.shape[0], fill, spare, on_rim)
    width_x, width_y, modes = dev.shape
    speed = courant[...]
    reach = jnp.abs(speed)
    ahead = jnp.where(speed > 0, 1.0, 0.0)
    if shards:
        edge = edges[0][0].astype(jnp.float32)
        before, after = jnp.where(where[0] == 1, edge, 0.0), jnp.where(where[0] == 0, edge, 0.0)
    else:
        before, after = edges[0][0].astype(jnp.float32), edges[1][0].astype(jnp.float32)
    lanes = 128
    moving = list(zip(fetches, stores))
    for low in range(0, modes, lanes):
        if low and moving:
            fetch, store = moving.pop(0)
            fetch.wait()
            store.start()
        cut = slice(low, low + lanes)
        a, b = reach[0:1, cut], reach[1:2, cut]
        stay_x, stay_y = 1.0 - a, 1.0 - b
        ahead_x = jnp.broadcast_to(ahead[0:1, cut], (width_y, lanes)) > 0
        ahead_y = jnp.broadcast_to(ahead[1:2, cut], (width_y, lanes)) > 0

        def one(x, behind, center, beyond):
            along = stay_x * center + a * jnp.where(ahead_x, behind, beyond)
            shifted = jnp.where(ahead_y, pltpu.roll(along, 1, 0), pltpu.roll(along, width_y - 1, 0))
            value = stay_y * along + b * shifted
            read[pl.ds(pl.multiple_of(x * width_y, 16), width_y), cut] = value.astype(read.dtype)

        def body(x, carry):
            behind, center = carry
            beyond = dev[x + 1, :, cut].astype(jnp.float32)
            one(x, behind, center, beyond)
            return center, beyond

        carry = (before[:, cut], dev[0, :, cut].astype(jnp.float32))
        behind, center = lax.fori_loop(0, width_x - 1, body, carry, unroll=4)
        one(width_x - 1, behind, center, after[:, cut])

    for fetch, store in moving:
        fetch.wait()
        store.start()
    head = read.shape[0] - extra.shape[0]
    tail_rows = read[head:, :]
    first = 0
    for out in outs:
        rows = slice(first, first + out.shape[0])
        first += out.shape[0]
        moved = jnp.dot(fill[rows, :], tail_rows, preferred_element_type=jnp.float32)
        kept = read[rows, :].astype(jnp.float32)
        out[...] = jnp.where(on_rim[rows, :] > 0, moved, kept).astype(out.dtype)
    extra[...] = jnp.dot(spare[...], tail_rows, preferred_element_type=jnp.float32).astype(extra.dtype)

    for store in stores:
        store.wait()


def payload_kernel(rows_of, cols_of, cells_lane, read, payload):
    slots, modes = payload.shape[2], read.shape[1]
    sub = jnp.broadcast_to(cells_lane[...], (128, slots)).T[:, 0:1]
    cell = lax.broadcasted_iota(jnp.int32, (slots, read.shape[0]), 1)
    select = (sub == cell).astype(jnp.float32).astype(jnp.bfloat16)
    rim = jnp.dot(select, read[...], preferred_element_type=jnp.float32)
    flipped = rim.T
    total = jnp.sum(flipped, axis=0, keepdims=True)
    high = total.astype(jnp.bfloat16).astype(jnp.float32)
    middle = (total - high).astype(jnp.bfloat16).astype(jnp.float32)
    low = total - high - middle
    place = lax.broadcasted_iota(jnp.int32, (TAIL, total.shape[1]), 0)
    tail = jnp.where(place == 0, high, jnp.where(place == 1, middle, jnp.where(place == 2, low, 0.0)))
    tail = tail.astype(jnp.bfloat16)
    piece = modes // (rows_of * cols_of)
    packed = flipped.astype(jnp.bfloat16)
    for r in range(rows_of):
        for c in range(cols_of):
            block = c * rows_of + r
            payload[r * cols_of + c, 0:piece, :] = packed[block * piece : (block + 1) * piece]
            payload[r * cols_of + c, piece : piece + TAIL, :] = tail


def rim_kernel(mode_count, specularity, arrived, mirror, wall, cells_lane, extra, out):
    groups, height, slots = arrived.shape
    piece = height - TAIL
    values = arrived[:, 0:piece, :].reshape(groups * piece, slots).T
    sums = arrived[:, piece:height, :].reshape(groups * TAIL, slots).astype(jnp.float32)
    total = jnp.broadcast_to(jnp.sum(sums, axis=0, keepdims=True), (128, slots)).T
    diffuse = total[:, 0:1] / mode_count
    walls = jnp.broadcast_to(wall[...], (128, slots)).T[:, 0:1]
    share = jnp.zeros(walls.shape, jnp.float32)
    mirrored = jnp.zeros(out.shape, jnp.float32)
    for w in range(mirror.shape[0]):
        share = jnp.where(walls == w, specularity[w], share)
        picked = jnp.dot(values, mirror[w], preferred_element_type=jnp.float32)
        mirrored = jnp.where(walls == w, picked, mirrored)
    emitted = share * mirrored + (1.0 - share) * diffuse
    used = jnp.broadcast_to(cells_lane[...], (128, slots)).T[:, 0:1] >= 0
    out[...] = jnp.where(used, emitted, extra[...].astype(jnp.float32)).astype(out.dtype)


def base_kernel(fill, on_rim, part, base):
    kept = part.shape[0]
    base[:kept, :] = jnp.where(on_rim[...] > 0, 0.0, part[...].astype(jnp.float32)).astype(base.dtype)
    moved = lax.dot_general(
        fill[...], part[...], (((0,), (0,)), ((), ())), preferred_element_type=jnp.float32
    )
    base[kept:, :] = moved.astype(base.dtype)


def merge_kernel(fill, spare, place, on_rim, base, total, from_left, from_right, out):
    slots = spare.shape[0]
    kept = base.shape[0] - slots
    total = total[...] + from_left[...].astype(jnp.float32) + from_right[...].astype(jnp.float32)
    total = total.astype(jnp.bfloat16)
    more = total.shape[0] - slots
    part, last = total[:more, :], total[more:, :]
    head = kept + more
    tn = (((0,), (0,)), ((), ()))
    moved = jnp.dot(place[:kept, :], last, preferred_element_type=jnp.float32)
    out[:kept, :] = (base[:kept, :].astype(jnp.float32) + moved).astype(out.dtype)
    moved = jnp.dot(place[kept:head, :], last, preferred_element_type=jnp.float32)
    out[kept:head, :] = jnp.where(on_rim[...] > 0, moved, part.astype(jnp.float32)).astype(out.dtype)
    moved = jnp.dot(place[head:, :], last, preferred_element_type=jnp.float32)
    moved = moved + lax.dot_general(spare[...], last, tn, preferred_element_type=jnp.float32)
    moved = moved + lax.dot_general(fill[...], part, tn, preferred_element_type=jnp.float32)
    out[head:, :] = (base[kept:, :].astype(jnp.float32) + moved).astype(out.dtype)


def hop_kernel(t, size, wide, slots, groups, has_recv, *refs):
    refs = list(refs)
    where = refs.pop(0)
    blocks = [[refs.pop(0) for _ in range(4)] for _ in range(groups)]
    own = refs.pop(0) if wide else None
    held = {j: (refs.pop(0), refs.pop(0)) for j in slots}
    final = t == size
    recv = [refs.pop(0), refs.pop(0)] if has_recv else None
    outs = [refs.pop(0)] if final else [refs.pop(0), refs.pop(0)]
    buffer, sem = refs
    s, r, c = where[0], where[1], where[2]
    rows = buffer.shape[1]
    width = blocks[0][0].shape[1]
    if final:
        jobs = [(c, None, size - 1)]
    else:
        first = slot_of(c, t, size)
        goes_right = c <= t - 1
        jobs = [
            (c + size - t, goes_right, first),
            (c - size + t, c >= size - t, first + jnp.where(goes_right, 1, 0)),
        ]

    def fetch(n, d, place):
        for b in range(4):
            source = lax.bitwise_xor(r, b)
            target = buffer.at[n, :, b * width : (b + 1) * width]
            if wide:
                column = pl.multiple_of(source * width, width)
                pltpu.make_async_copy(
                    own.at[pl.ds(pl.multiple_of(d * rows, rows), rows), pl.ds(column, width)],
                    target,
                    sem.at[n],
                ).start()
                continue
            column = pl.multiple_of(lax.bitwise_and(source, 1) * width, width)
            is_own = lax.shift_right_logical(source, 1) == s
            for j, pair in held.items():
                for use, shard in ((is_own, pair[0]), (jnp.logical_not(is_own), pair[1])):

                    @pl.when(jnp.logical_and(use, place == j))
                    def _(shard=shard):
                        pltpu.make_async_copy(shard.at[:, pl.ds(column, width)], target, sem.at[n]).start()

    def multiply(n, out):
        pltpu.make_async_copy(buffer.at[n], buffer.at[n], sem.at[n]).wait()
        first = 0
        for group in blocks:
            height = group[0].shape[0]
            tile = min(384, height)

            def rows_of_tile(i, carry, group=group, first=first, tile=tile):
                low = pl.multiple_of(i * tile, tile)
                inside, rows_here = pl.ds(low, tile), pl.ds(first + low, tile)
                total = None
                for b in range(4):
                    part = lax.dot_general(
                        group[b][inside, :],
                        buffer[n, :, b * width : (b + 1) * width],
                        NT,
                        preferred_element_type=jnp.float32,
                    )
                    total = part if total is None else total + part
                if final and has_recv:
                    total = total + recv[0][rows_here, :].astype(jnp.float32)
                    total = total + recv[1][rows_here, :].astype(jnp.float32)
                elif has_recv:
                    total = total + recv[n][rows_here, :].astype(jnp.float32)
                out[rows_here, :] = total.astype(out.dtype)
                return carry

            lax.fori_loop(0, height // tile, rows_of_tile, 0)
            first += height

    for n, (d, valid, place) in enumerate(jobs):
        if valid is None:
            fetch(n, d, place)
        else:
            pl.when(valid)(functools.partial(fetch, n, d, place))
    for n, (d, valid, place) in enumerate(jobs):
        if valid is None:
            multiply(n, outs[n])
        else:
            pl.when(valid)(functools.partial(multiply, n, outs[n]))


def hop(t, size, where, blocks, own, held, recv):
    wide = own is not None
    slots = () if wide else tuple(slots_at(t, size))
    rows = own.shape[0] // size if wide else held[0][0].shape[0]
    cells = sum(group[0].shape[0] for group in blocks)
    width = blocks[0][0].shape[1]
    count = 1 if t == size else 2
    kept = jnp.float32 if t == size and recv is None else jnp.bfloat16
    spec = pl.BlockSpec(memory_space=pltpu.VMEM)
    any_spec = pl.BlockSpec(memory_space=HBM)
    shards = [own] if wide else [shard for j in slots for shard in held[j]]
    operands = [where, *[block for group in blocks for block in group], *shards, *(recv or [])]
    in_specs = [pl.BlockSpec(memory_space=SMEM)] + [spec] * (4 * len(blocks)) + [any_spec] * len(shards)
    in_specs += [spec] * len(recv or [])
    return pl.pallas_call(
        functools.partial(hop_kernel, t, size, wide, slots, len(blocks), recv is not None),
        out_shape=[jax.ShapeDtypeStruct((cells, rows), kept)] * count,
        in_specs=in_specs,
        out_specs=[spec] * count,
        scratch_shapes=[
            pltpu.VMEM((count, rows, 4 * width), jnp.bfloat16),
            pltpu.SemaphoreType.DMA((count,)),
        ],
        compiler_params=pltpu.CompilerParams(vmem_limit_bytes=HOP_LIMIT),
        cost_estimate=takes(2 + cells / 300),
    )(*operands)


def on_device(deviation, courant, collide, hole_cells, hole_wall, specular, specularity):
    n_space, n_row, n_col = (lax.axis_size(name) for name in ("space", "mrow", "mcol"))
    s, r, c = (lax.axis_index(name) for name in ("space", "mrow", "mcol"))
    width_x, width_y, block_len = deviation.shape
    cell_count = width_x * width_y
    slot_count = hole_cells.shape[0]
    wall_count, mode_count = specular.shape
    piece = block_len // (n_row * n_col)
    groups = n_row * n_col
    vmem = pl.BlockSpec()
    hbm = pl.BlockSpec(memory_space=HBM)
    smem = pl.BlockSpec(memory_space=SMEM)
    params = pltpu.CompilerParams(vmem_limit_bytes=LIMIT)
    roomy = pltpu.CompilerParams(vmem_limit_bytes=24 * 1024 * 1024)
    where = jnp.stack([s, r, c]).astype(jnp.int32)

    if n_space == 2:
        edge = jnp.where(s == 0, deviation[-1:], deviation[:1])
        edges = [lax.ppermute(edge, "space", [(0, 1), (1, 0)])]
    else:
        up = [(i, i + 1) for i in range(n_space - 1)]
        down = [(j, i) for i, j in up]
        edges = [lax.ppermute(deviation[-1:], "space", up), lax.ppermute(deviation[:1], "space", down)]

    def after(value, *first):
        return lax.optimization_barrier((value, first))[0]

    def shape(*dims):
        return jax.ShapeDtypeStruct(dims, jnp.bfloat16)

    head = cell_count - slot_count
    sizes = [head * part // sum(SPLIT) for part in SPLIT]
    count = len(sizes)
    lane_cells = hole_cells[None, :]
    wide = n_space != 2
    rows = collide.shape[0] // n_col
    own = lax.all_gather(collide, "space", axis=1, tiled=True) if wide else None
    shards = 0 if wide else n_col
    swap = [(0, 1), (1, 0)]
    held, order = [], jnp.asarray(line_steps(n_col))
    extra, *mine = pl.pallas_call(
        functools.partial(read_kernel, count, shards),
        out_shape=[shape(slot_count, block_len)]
        + [shape(size, block_len) for size in sizes]
        + [shape(rows, collide.shape[1])] * shards
        + [shape(cell_count, block_len)],
        in_specs=[smem] + [vmem] * (3 + len(edges)) + [smem, hbm][: shards * 2],
        out_specs=[vmem] * (count + 1) + [hbm] * shards + [vmem],
        scratch_shapes=[
            pltpu.VMEM((head, slot_count), jnp.bfloat16),
            pltpu.VMEM((slot_count, slot_count), jnp.bfloat16),
            pltpu.VMEM((head, 1), jnp.float32),
        ]
        + [
            pltpu.VMEM((shards, rows, collide.shape[1]), jnp.bfloat16),
            pltpu.SemaphoreType.DMA((shards,)),
            pltpu.SemaphoreType.DMA((shards,)),
        ][: shards * 3],
        compiler_params=params,
        cost_estimate=takes(6),
    )(where, deviation, courant, hole_cells, *edges, *([] if wide else [order, collide]))
    read = mine.pop()
    payload = pl.pallas_call(
        functools.partial(payload_kernel, n_row, n_col),
        out_shape=shape(groups, piece + TAIL, slot_count),
        in_specs=[vmem] * 2,
        out_specs=vmem,
        compiler_params=params,
        cost_estimate=takes(3),
    )(lane_cells, read)
    mine, parts = mine[:count], mine[count:]
    for part in parts:
        held.append((part, lax.ppermute(part, "space", swap)))

    flip = [[(i, i ^ bit) for i in range(n_row)] for bit in (1, 2)]
    right = [(i, i + 1) for i in range(n_col - 1)]
    left = [(j, i) for i, j in right]
    far = []
    for value in mine:
        far.append(lax.ppermute(value, "mrow", flip[1]))
    arrived = lax.all_to_all(payload, ("mrow", "mcol"), split_axis=0, concat_axis=0, tiled=True)
    def send(t, value):
        return [
            lax.ppermute(value[0], "mcol", right[:t]),
            lax.ppermute(value[1], "mcol", left[n_col - 1 - t :]),
        ]

    state = {}
    done = ()

    def step(t, n, *ready):
        return hop(t, n_col, after(where, *done, *ready), chunks[n], own, held, state.get(n))

    def gather(n):
        near = lax.ppermute(mine[n], "mrow", flip[0])
        both = lax.ppermute(after(far[n], *done), "mrow", flip[0])
        return [mine[n], near, far[n], both]

    own_table = lax.dynamic_slice_in_dim(specular, (c * n_row + r) * block_len, block_len, 1)
    mirror, place, spare, fill, fill_more, on_rim, on_rim_more = pl.pallas_call(
        functools.partial(late_mask_kernel, n_row, n_col),
        out_shape=[
            shape(wall_count, block_len, block_len),
            shape(cell_count, slot_count),
            shape(slot_count, slot_count),
            *[shape(size, slot_count) for size in sizes],
            *[jax.ShapeDtypeStruct((size, 1), jnp.float32) for size in sizes],
        ],
        in_specs=[vmem] * 2,
        out_specs=[vmem] * 7,
        scratch_shapes=[pltpu.VMEM((head, slot_count), jnp.bfloat16), pltpu.VMEM((head, 1), jnp.float32)],
        compiler_params=params,
        cost_estimate=takes(4),
    )(after(lane_cells, extra), own_table)
    far[0] = after(far[0], mirror, *[other for _, other in held[:1]])
    chunks = [[gather(0)]]
    done = step(1, 0, arrived)
    state[0] = send(1, done)
    mine.append(
        pl.pallas_call(
            functools.partial(rim_kernel, mode_count),
            out_shape=shape(slot_count, block_len),
            in_specs=[smem] + [vmem] * 5,
            out_specs=vmem,
            compiler_params=roomy,
            cost_estimate=takes(4),
        )(specularity, after(arrived, far[1], *done), mirror, hole_wall[None, :], lane_cells, extra)
    )
    far.append(lax.ppermute(mine[count], "mrow", flip[1]))
    chunks.append([gather(n) for n in range(1, count + 1)])
    done = step(1, 1, *state[0])
    state[1] = send(1, done)
    outs = []
    for t in range(2, n_col + 1):
        for n in (0, 1):
            if (t, n) == (n_col, 1):
                continue
            done = step(t, n)
            if t == n_col:
                outs.append(done[0])
            else:
                state[n] = send(t, done)
    total = hop(n_col, n_col, after(where, *done), chunks[1], own, held, None)[0]
    base = pl.pallas_call(
        base_kernel,
        out_shape=shape(sizes[0] + slot_count, rows),
        in_specs=[vmem] * 3,
        out_specs=vmem,
        compiler_params=roomy,
        cost_estimate=takes(2),
    )(fill, on_rim, *outs)
    near = pl.BlockSpec(memory_space=pltpu.VMEM)
    out = pl.pallas_call(
        merge_kernel,
        out_shape=shape(cell_count, rows),
        in_specs=[near] * 8,
        out_specs=vmem,
        compiler_params=pltpu.CompilerParams(vmem_limit_bytes=HOP_LIMIT),
        cost_estimate=takes(4),
    )(fill_more, spare, place, on_rim_more, base, total, *state[1])
    return out.reshape(width_x, width_y, rows)


def solution(mesh):
    in_specs = (
        P("space", None, ("mcol", "mrow")),
        P(None, ("mcol", "mrow")),
        P("mrow", ("mcol", "space")),
        P("space"),
        P("space"),
        P(),
        P(),
    )
    out_specs = P("space", None, ("mrow", "mcol"))
    return jax.shard_map(
        on_device, mesh=mesh, in_specs=in_specs, out_specs=out_specs, check_vma=False
    )
```
